256 devices in a mesh: wave: 16 (over y, z_hi), ty: 4 (over z_lo, core), tx: 4 (over x).
Axes of the slice: x: 4, y: 4, z: 8 (z_hi: 4, z_lo: 2; z = z_hi * 2 + z_lo), core: 2. Of those that a mesh axis runs over, the one named last changes fastest.
Arguments:
- object_field: float32 [2, 2048, 2048], P(None, 'ty', 'tx'), may hold values from -5 to 5
- probes: float32 [16, 2, 256, 256], P('wave'), may hold values from -5 to 5
- measured: float32 [4, 4, 8, 256, 256], P('ty', 'tx'), may hold values from 0.1 to 4
- positions: int32 [4, 4, 8, 2], P('ty', 'tx'), may hold values from 0 to 256, as said below
- weights: float32 [16], P('wave'), may hold values from 0.5 to 12, as said below
Outputs:
- new_object: float32 [2, 2048, 2048], P(None, 'ty', 'tx')
- new_probes: float32 [16, 2, 256, 256], P('wave')
The draws below stay inside these ranges and needn't reach their ends.
Inputs may be any that keep to these rules, and one draw needn't show every extreme that they name: `positions`: each frame lies wholly inside its tile; some offset equals 0 and some equals 256. Positive weights.
All inputs are finite; a program needn't handle non-finite values.
Results may differ from the reference program's by a relative error of at most 0.0003.
Values sent between devices are 32-bit elements; how exact they have to be, the bound alone decides.
No kernel may reach another device: no remote copies, remote signals or barrier semaphores. Data moves between devices by JAX's collectives and lax.ppermute only.
A program may use at most 64 MiB of HBM per device.

```python
import math
import jax
import jax.numpy as jnp
from jax import lax

P_SIZE = 256
TILE = 512
FRAMES = 8
WAVES = 16
ROWS_T = 4
COLS_T = 4
NY = 2048
NX = 2048


def draw_positions(key, part):
    first, second, third = jax.random.split(jax.random.fold_in(key, 17), 3)
    total = ROWS_T * COLS_T * FRAMES * 2
    flat = jax.random.randint(first, (total,), 0, TILE - P_SIZE + 1)
    lowest = jax.random.randint(second, (), 0, total)
    stride = jax.random.randint(third, (), 1, total)
    highest_at = (lowest + stride) % total
    flat = flat.at[lowest].set(0)
    flat = flat.at[highest_at].set(TILE - P_SIZE)
    return flat.reshape(ROWS_T, COLS_T, FRAMES, 2).astype(jnp.int32)


def draw_weights(key, part):
    ramp = 1.0 + 2.0 * jnp.arange(WAVES, dtype=jnp.float32) / max(WAVES - 1, 1)
    jitter = jax.random.uniform(jax.random.fold_in(key, 29), (WAVES,), jnp.float32, 0.7, 1.3)
    values = ramp * jitter
    return values.astype(jnp.float32)


def level_of(own_key, extent, pieces, low, high):
    factor_of, own = 1.0, jax.random.fold_in(own_key, 6)
    for position, parts in pieces:
        steps = jnp.exp(jax.random.uniform(jax.random.fold_in(own, position), (parts,), jnp.float32, low / len(pieces), high / len(pieces)))
        factor_of = factor_of * jnp.repeat(steps, extent[position] // parts).reshape([-1 if axis == position else 1 for axis in range(len(extent))])
    return factor_of


def noise(rng, extent, spread, bound, cuts=(), held_as=jnp.bfloat16):
    entries = spread * jax.random.normal(rng, extent, jnp.float32)
    if cuts:
        entries = entries * level_of(rng, extent, cuts, -0.22, 0.18)
    return jnp.clip(entries, -bound, bound).astype(held_as)


def setup_inputs(seed: int = 0) -> dict:
    arg_keys = jax.random.split(jax.random.key(seed), 6)
    return {
        "object_field": noise(arg_keys[0], (2, NY, NX), 0.7, 5.0, ((1, 4), (2, 4)), jnp.float32),
        "probes": noise(arg_keys[1], (WAVES, 2, P_SIZE, P_SIZE), 0.7, 5.0, ((0, 16),), jnp.float32),
        "measured": jnp.clip(jnp.exp(math.log(4.0) - 3.6888794 * jax.random.uniform(arg_keys[2], (ROWS_T, COLS_T, FRAMES, P_SIZE, P_SIZE), jnp.float32) ** level_of(arg_keys[2], (ROWS_T, COLS_T, FRAMES, P_SIZE, P_SIZE), ((0, 4), (1, 4)), -0.2, 0.2)), 0.1, 4.0),
        "positions": draw_positions(jax.random.fold_in(arg_keys[5], 71), 0),
        "weights": draw_weights(jax.random.fold_in(arg_keys[5], 71), 0),
    }


highest = lax.Precision.HIGHEST
damping = 1.0
intensity_offset = 0.1

def tables(length):
    indices = jnp.arange(length, dtype=jnp.int32)
    product = indices[:, None] * indices[None, :] % length
    angles = 2.0 * math.pi / length * product.astype(jnp.float32)
    norm_scale = 1.0 / math.sqrt(length)
    return (jnp.cos(angles) * norm_scale, -jnp.sin(angles) * norm_scale)

def transform(real_part, imag_part, cosine_table, sine_table):
    left_real = jnp.matmul(cosine_table, real_part, precision=highest) - jnp.matmul(sine_table, imag_part, precision=highest)
    left_imag = jnp.matmul(cosine_table, imag_part, precision=highest) + jnp.matmul(sine_table, real_part, precision=highest)
    out_real = jnp.matmul(left_real, cosine_table, precision=highest) - jnp.matmul(left_imag, sine_table, precision=highest)
    out_imag = jnp.matmul(left_real, sine_table, precision=highest) + jnp.matmul(left_imag, cosine_table, precision=highest)
    return (out_real, out_imag)

def tile_update(tile_field, probe_real, probe_imag, illumination, measured_tile, offsets, weights, total_weight, cosine_table, sine_table):
    anchor = jnp.zeros((), jnp.int32)
    patches = jnp.stack([lax.dynamic_slice(tile_field, (anchor, offsets[frame_idx, 0], offsets[frame_idx, 1]), (2, P_SIZE, P_SIZE)) for frame_idx in range(FRAMES)])
    obj_real = patches[:, 0][None]
    obj_imag = patches[:, 1][None]
    exit_real = probe_real * obj_real - probe_imag * obj_imag
    exit_imag = probe_real * obj_imag + probe_imag * obj_real
    wave_real, wave_imag = transform(exit_real, exit_imag, cosine_table, sine_table)
    power_sum = lax.optimization_barrier(jnp.sum(weights[:, None, None, None] * (wave_real * wave_real + wave_imag * wave_imag), axis=0))
    model_power = power_sum / total_weight
    factor = jnp.sqrt(measured_tile) / jnp.sqrt(model_power + intensity_offset) - 1.0
    diff_real, diff_imag = transform(wave_real * factor, wave_imag * factor, cosine_table, -sine_table)
    grad_real = lax.optimization_barrier(jnp.sum(probe_real * diff_real + probe_imag * diff_imag, axis=0))
    grad_imag = lax.optimization_barrier(jnp.sum(probe_real * diff_imag - probe_imag * diff_real, axis=0))
    gradient_sum = jnp.zeros((3, TILE, TILE), jnp.float32)
    for frame_idx in range(FRAMES):
        corner = (anchor, offsets[frame_idx, 0], offsets[frame_idx, 1])
        current = lax.dynamic_slice(gradient_sum, corner, (3, P_SIZE, P_SIZE))
        addition = jnp.stack([grad_real[frame_idx], grad_imag[frame_idx], illumination])
        gradient_sum = lax.dynamic_update_slice(gradient_sum, current + addition, corner)
    new_tile = tile_field + gradient_sum[:2] / (gradient_sum[2:3] + damping)
    probe_grad_real = lax.optimization_barrier(jnp.sum(obj_real * diff_real + obj_imag * diff_imag, axis=1))
    probe_grad_imag = lax.optimization_barrier(jnp.sum(obj_real * diff_imag - obj_imag * diff_real, axis=1))
    denominator = lax.optimization_barrier(jnp.sum(obj_real[0] * obj_real[0] + obj_imag[0] * obj_imag[0], axis=0))
    return (new_tile, jnp.stack([probe_grad_real, probe_grad_imag], axis=1), denominator)

def reference(object_field, probes, measured, positions, weights):
    cosine_table, sine_table = tables(P_SIZE)
    total_weight = jnp.sum(weights)
    probe_real = probes[:, 0][:, None]
    probe_imag = probes[:, 1][:, None]
    illumination = lax.optimization_barrier(jnp.sum(probes[:, 0] * probes[:, 0] + probes[:, 1] * probes[:, 1], axis=0))
    anchor = jnp.zeros((), jnp.int32)

    def per_tile(carry, tile_index):
        row_tile = tile_index // COLS_T
        col_tile = tile_index % COLS_T
        tile_field = lax.dynamic_slice(object_field, (anchor, row_tile * TILE, col_tile * TILE), (2, TILE, TILE))
        new_tile, probe_grad, denominator = tile_update(tile_field, probe_real, probe_imag, illumination, measured[row_tile, col_tile], positions[row_tile, col_tile], weights, total_weight, cosine_table, sine_table)
        return ((carry[0] + probe_grad, carry[1] + denominator), new_tile)
    start = (jnp.zeros((WAVES, 2, P_SIZE, P_SIZE), jnp.float32), jnp.zeros((P_SIZE, P_SIZE), jnp.float32))
    (probe_grad, denominator), new_tiles = lax.scan(per_tile, start, jnp.arange(ROWS_T * COLS_T, dtype=jnp.int32))
    new_tiles = new_tiles.reshape(ROWS_T, COLS_T, 2, TILE, TILE).transpose(2, 0, 3, 1, 4).reshape(2, NY, NX)
    new_probes = probes + probe_grad / (denominator + damping)
    return (new_tiles, new_probes)
```

```python
import math

import jax
import jax.numpy as jnp
import ml_dtypes
import numpy as np
from jax import lax
from jax.experimental import pallas as pl
from jax.experimental.pallas import tpu as pltpu
from jax.sharding import Mesh
from jax.sharding import PartitionSpec as P

f32 = jnp.float32
bf16 = jnp.bfloat16
damping = 1.0
intensity_offset = 0.1
N = 256
SIDE = 512
TALL = 264
VMEM_LIMIT = 48 * 1024 * 1024


def tables():
    k = np.arange(N)
    angle = 2.0 * math.pi / N * (np.outer(k, k) % N)
    c = np.cos(angle) / math.sqrt(N)
    s = -np.sin(angle) / math.sqrt(N)

    def split(table):
        high = table.astype(np.float32).astype(ml_dtypes.bfloat16)
        low = (table - high.astype(np.float64)).astype(np.float32).astype(ml_dtypes.bfloat16)
        return np.concatenate([high, high, low], axis=1)

    forward = split(np.block([[c, -s], [s, c]]))
    inverse = split(np.block([[c, s], [-s, c]]))
    return forward, inverse


def half_transform(re, im, table):
    x = jnp.concatenate([re, im], axis=1)
    high = x.astype(bf16)
    low = (x - high.astype(f32)).astype(bf16)
    data = jnp.concatenate([high, low, high], axis=1)
    out = lax.dot_general(table, data, (((1,), (1,)), ((), ())), preferred_element_type=f32)
    return out[:N], out[N:]


def transform(re, im, table):
    re, im = half_transform(re, im, table)
    return half_transform(re, im, table)


def split_row(row):
    base = pl.multiple_of(jnp.minimum(row // 8 * 8, SIDE - TALL), 8)
    return base, row - base


def spec(space=pltpu.VMEM):
    return pl.BlockSpec(memory_space=space)


def call(kernel, name, ins, outs, scratch=(), flops=0, nbytes=0):
    return pl.pallas_call(
        kernel,
        name=name,
        out_shape=[jax.ShapeDtypeStruct(o, f32) for o in outs],
        in_specs=ins,
        out_specs=[spec() for _ in outs],
        scratch_shapes=list(scratch),
        compiler_params=pltpu.CompilerParams(vmem_limit_bytes=VMEM_LIMIT),
        cost_estimate=pl.CostEstimate(flops=flops, bytes_accessed=nbytes, transcendentals=0),
    )


V = spec()
S = spec(pltpu.SMEM)
MiB = 1 << 20


def first_kernel(where, positions, weight, obj, probe, table, patches, power, total, psi):
    w = weight[0]
    lit = jnp.zeros((N, N), f32)
    for f in range(2):
        base, down = split_row(positions[2 * where[0] + f, 0])
        col = positions[2 * where[0] + f, 1]
        parts = []
        for ch in range(2):
            rows = obj[ch, pl.ds(base, TALL), :]
            part = pltpu.roll(rows, lax.rem(SIDE - col, SIDE), 1)[:, :N]
            part = pltpu.roll(part, lax.rem(TALL - down, TALL), 0)[:N]
            patches[f, ch] = part
            parts.append(part)
        o_re, o_im = parts
        lit = lit + (o_re * o_re + o_im * o_im)
        p_re, p_im = probe[0], probe[1]
        re, im = transform(p_re * o_re - p_im * o_im, p_re * o_im + p_im * o_re, table[...])
        psi[f, 0] = re
        psi[f, 1] = im
        power[f] = w * (re * re + im * im)
    total[...] = lit


def second_kernel(where, weight, patches, probe, power0, a1, a2, a3, b1, b2, b3, table,
                  out0, out1, out2, out3, psi, probes, power):
    zh, c, x = where[1], where[2], where[3]
    power[...] = power0[...]
    wsum = jnp.full((8, N), weight[0], f32)
    flag = jnp.full((1, N), c, jnp.int32) == 0
    for i, (a, b) in enumerate(((a1, b1), (a2, b2), (a3, b3))):
        own, other = a[:N, :], b[:N, :]
        probes[i, 0] = jnp.where(flag, own, other)
        probes[i, 1] = jnp.where(flag, other, own)
        wsum = wsum + a[N:, :]
    for i, a in enumerate((a1, a2, a3)):
        w = a[N:N + 1, :]
        for f in range(2):
            p_re, p_im = probes[i, 0], probes[i, 1]
            o_re, o_im = patches[f, 0], patches[f, 1]
            re, im = transform(p_re * o_re - p_im * o_im, p_re * o_im + p_im * o_re, table[...])
            psi[i, f, 0] = re
            psi[i, f, 1] = im
            power[f] += w * (re * re + im * im)
    for s, out in enumerate((out0, out1, out2, out3)):
        j = lax.rem(zh + s, 4)
        out[:128, :] = power[j // 2, pl.ds(pl.multiple_of((j % 2) * 128, 128), 128), :]
        out[128:136, :] = wsum
        rows = pl.ds(pl.multiple_of(32 * (2 * x + c) + 8 * j, 8), 8)
        re, im = probe[0, rows, :], probe[1, rows, :]
        light = re * re + im * im
        for i in range(3):
            re, im = probes[i, 0, rows, :], probes[i, 1, rows, :]
            light = light + (re * re + im * im)
        out[136:144, :] = light


def factor_kernel(m0, m1, m2, m3, measured, out):
    total = (m0[...] + m1[...]) + (m2[...] + m3[...])
    model = total[:128] / total[128:129]
    out[:128, :] = jnp.sqrt(measured[...]) / jnp.sqrt(model + intensity_offset) - 1.0
    out[128:, :] = total[136:]


def third_kernel(where, positions, f0, f1, f2, f3, patches, lit, probe, probes, psi0, psi, table,
                 g0, g1, g2, g3, keep, send, factor, canvas, q):
    y, zh, c = where[0], where[1], where[2]
    for s, f in enumerate((f0, f1, f2, f3)):
        factor[lax.rem(zh + 4 - s, 4)] = f[:128, :]
    canvas[...] = jnp.zeros_like(canvas)
    for f in range(2):
        fac = jnp.concatenate([factor[2 * f], factor[2 * f + 1]], axis=0)
        o_re, o_im = patches[f, 0], patches[f, 1]
        g_re = jnp.zeros((N, N), f32)
        g_im = jnp.zeros((N, N), f32)
        for i in range(4):
            a_re, a_im = (psi0[f, 0], psi0[f, 1]) if i == 0 else (psi[i - 1, f, 0], psi[i - 1, f, 1])
            p_re, p_im = (probe[0], probe[1]) if i == 0 else (probes[i - 1, 0], probes[i - 1, 1])
            re, im = transform(a_re * fac, a_im * fac, table[...])
            g_re = g_re + (p_re * re + p_im * im)
            g_im = g_im + (p_re * im - p_im * re)
            q_re = o_re * re + o_im * im
            q_im = o_re * im - o_im * re
            if f == 0:
                q[0, i] = q_re
                q[1, i] = q_im
            else:
                q[0, i] += q_re
                q[1, i] += q_im
        base, down = split_row(positions[2 * y + f, 0])
        col = positions[2 * y + f, 1]
        for ch, g in enumerate((g_re, g_im)):
            tall = pltpu.roll(jnp.concatenate([g, jnp.zeros((TALL - N, N), f32)], axis=0), down, 0)
            wide = pltpu.roll(jnp.concatenate([tall, jnp.zeros((TALL, N), f32)], axis=1), col, 1)
            canvas[ch, pl.ds(base, TALL), :] += wide
    for s, out in enumerate((g0, g1, g2, g3)):
        start = pl.multiple_of(lax.rem(y + s, 4) * 128, 128)
        for ch in range(2):
            out[ch] = canvas[ch, pl.ds(start, 128), :]
    for xc in range(4):
        for i in range(4):
            keep[xc, 64 * i:64 * i + 64, :] = q[c, i, 64 * xc:64 * xc + 64, :]
            send[xc, 64 * i:64 * i + 64, :] = q[1 - c, i, 64 * xc:64 * xc + 64, :]
        keep[xc, 256:, :] = lit[64 * xc:64 * xc + 64, :]
        send[xc, 256:, :] = lit[64 * xc:64 * xc + 64, :]


def sum_kernel(where, g0, g1, g2, g3, o0, o1, o2, o3):
    for s, out in enumerate((o0, o1, o2, o3)):
        rows = pl.ds(pl.multiple_of(lax.rem(where[1] + s, 4) * 32, 32), 32)
        for ch in range(2):
            out[ch] = (g0[ch, rows, :] + g1[ch, rows, :]) + (g2[ch, rows, :] + g3[ch, rows, :])


def light_kernel(where, positions, light, out, padded):
    padded[:32, :] = jnp.zeros((32, N), f32)
    padded[32:288, :] = light[...]
    padded[288:328, :] = jnp.zeros((40, N), f32)
    first = 128 * where[0] + 32 * where[1]
    total = jnp.zeros((32, SIDE), f32)
    for f in range(8):
        start = jnp.clip(first - positions[f, 0] + 32, 0, 288)
        base = start // 8 * 8
        rows = padded[pl.ds(pl.multiple_of(base, 8), 40), :]
        rows = pltpu.roll(rows, lax.rem(40 - (start - base), 40), 0)[:32]
        wide = jnp.concatenate([rows, jnp.zeros((32, N), f32)], axis=1)
        total = total + pltpu.roll(wide, positions[f, 1], 1)
    out[...] = total


def update_kernel(o0, o1, o2, o3, obj, light, out):
    scale = light[...] + damping
    for ch in range(2):
        out[ch] = obj[ch] + ((o0[ch] + o1[ch]) + (o2[ch] + o3[ch])) / scale


def shift(x, axis, n, s):
    return lax.ppermute(x, axis, [(i, (i + s) % n) for i in range(n)])


def ordered(parts, index, axis=0):
    n = len(parts)
    stacked = jnp.stack(parts, axis)
    order = [lax.rem(index + n - j, n) for j in range(n)]
    return jnp.stack([lax.dynamic_index_in_dim(stacked, o, axis, False) for o in order], axis)


def local(object_field, probes, measured, positions, weights):
    forward, inverse = (jnp.asarray(t) for t in tables())
    y, zh, c, x = (lax.axis_index(a) for a in ("y", "zh", "c", "x"))
    where = jnp.stack([y, zh, c, x]).astype(jnp.int32)
    offsets = positions[0, 0]
    probe = probes[0]

    own = lax.dynamic_index_in_dim(probe, c, 0, False)
    message = jnp.concatenate([own, jnp.broadcast_to(weights[:, None], (8, N))], axis=0)
    near = [shift(message, "y", 4, s) for s in (1, 2, 3)]
    far = [shift(m, "c", 2, 1) for m in near]

    plane = (N, N)
    patches, power0, lit, psi0 = call(
        first_kernel, "first", [S, S, S, V, V, V],
        [(2, 2) + plane, (2,) + plane, plane, (2, 2) + plane], flops=5 * 10**9, nbytes=6 * MiB,
    )(where, offsets, weights, object_field, probe, forward)

    *sums, psi, others = call(
        second_kernel, "second", [S, S] + [V] * 10,
        [(144, N)] * 4 + [(3, 2, 2) + plane, (3, 2) + plane],
        [pltpu.VMEM((2,) + plane, f32)], flops=15 * 10**9, nbytes=10 * MiB,
    )(where, weights, patches, probe, power0, *near, *far, forward)

    got = [sums[0]] + [shift(sums[s], "zh", 4, s) for s in (1, 2, 3)]
    mine = lax.dynamic_index_in_dim(measured.reshape(16, 128, N), 4 * y + zh, 0, False)
    (factor,) = call(factor_kernel, "factor", [V] * 5, [(136, N)], flops=10**6, nbytes=MiB)(*got, mine)
    factors = [factor] + [shift(factor, "zh", 4, s) for s in (1, 2, 3)]

    *grads, keep, send = call(
        third_kernel, "third", [S, S] + [V] * 11,
        [(2, 128, SIDE)] * 4 + [(4, 320, N)] * 2,
        [pltpu.VMEM((4, 128, N), f32), pltpu.VMEM((2, SIDE, SIDE), f32), pltpu.VMEM((2, 4) + plane, f32)],
        flops=20 * 10**9, nbytes=14 * MiB,
    )(where, offsets, *factors, patches, lit, probe, others, psi0, psi, inverse)

    got = [grads[0]] + [shift(grads[s], "y", 4, s) for s in (1, 2, 3)]

    rows = ordered([f[128:] for f in factors], zh).reshape(32, N)
    rows = ordered([rows] + [shift(rows, "x", 4, s) for s in (1, 2, 3)], x)
    rows = ordered([rows, shift(rows, "c", 2, 1)], c, 1)
    (light,) = call(
        light_kernel, "light", [S, S, V], [(32, SIDE)], [pltpu.VMEM((328, N), f32)],
        flops=10**6, nbytes=MiB,
    )(where, offsets, rows.reshape(N, N))

    sums = call(sum_kernel, "sum", [S] + [V] * 4, [(2, 32, SIDE)] * 4, flops=10**6, nbytes=3 * MiB)(where, *got)
    got = [sums[0]] + [shift(sums[s], "zh", 4, s) for s in (1, 2, 3)]
    mine = lax.dynamic_index_in_dim(object_field.reshape(2, 16, 32, SIDE), 4 * y + zh, 1, False)
    (new,) = call(update_kernel, "update", [V] * 6, [(2, 32, SIDE)], flops=10**6, nbytes=MiB)(*got, mine, light)
    block = ordered([new] + [shift(new, "zh", 4, s) for s in (1, 2, 3)], zh, 1).reshape(2, 128, SIDE)
    tile = ordered([block] + [shift(block, "y", 4, s) for s in (1, 2, 3)], y, 1)
    new_object = tile.reshape(2, SIDE, SIDE)

    both = keep + shift(send, "c", 2, 1)
    parts = [lax.dynamic_index_in_dim(both, lax.rem(x + s, 4), 0, False) for s in range(4)]
    q = parts[0] + sum(shift(parts[s], "x", 4, s) for s in (1, 2, 3))
    e = q[256:]
    parts = [jnp.concatenate([q[64 * s:64 * s + 64], e]) for s in range(4)]
    q = parts[0] + sum(shift(parts[s], "y", 4, -s) for s in (1, 2, 3))
    q = q + shift(q, "zl", 2, 1)
    mine = lax.dynamic_slice(probe, (c, 64 * x, 0), (1, 64, N))[0]
    new = mine + q[:64] / (q[64:] + damping)
    half = ordered([new] + [shift(new, "x", 4, s) for s in (1, 2, 3)], x).reshape(N, N)
    new_probe = ordered([half, shift(half, "c", 2, 1)], c)
    return new_object, new_probe[None]


def solution(mesh):
    inner = Mesh(mesh.devices.reshape(4, 4, 2, 2, 4), ("y", "zh", "zl", "c", "x"))
    wave, ty, tx = ("y", "zh"), ("zl", "c"), "x"
    in_specs = (
        P(None, ty, tx),
        P(wave, None, None, None),
        P(ty, tx, None, None, None),
        P(ty, tx, None, None),
        P(wave),
    )
    out_specs = (P(None, ty, tx), P(wave, None, None, None))
    return jax.shard_map(local, mesh=inner, in_specs=in_specs, out_specs=out_specs, check_vma=False)
```

```python
import math

import jax
import jax.numpy as jnp
import ml_dtypes
import numpy as np
from jax import lax
from jax.experimental import pallas as pl
from jax.experimental.pallas import tpu as pltpu
from jax.sharding import Mesh
from jax.sharding import PartitionSpec as P

f32 = jnp.float32
bf16 = jnp.bfloat16
damping = 1.0
intensity_offset = 0.1
N = 256
SIDE = 512
TALL = 264
VMEM_LIMIT = 48 * 1024 * 1024


def tables():
    k = np.arange(N)
    angle = 2.0 * math.pi / N * (np.outer(k, k) % N)
    c = np.cos(angle) / math.sqrt(N)
    s = -np.sin(angle) / math.sqrt(N)

    def split(table):
        high = table.astype(np.float32).astype(ml_dtypes.bfloat16)
        low = (table - high.astype(np.float64)).astype(np.float32).astype(ml_dtypes.bfloat16)
        return np.concatenate([high, high, low], axis=1)

    forward = split(np.block([[c, -s], [s, c]]))
    inverse = split(np.block([[c, s], [-s, c]]))
    return forward, inverse


def half_transform(re, im, table):
    x = jnp.concatenate([re, im], axis=1)
    high = x.astype(bf16)
    low = (x - high.astype(f32)).astype(bf16)
    data = jnp.concatenate([high, low, high], axis=1)
    out = lax.dot_general(table, data, (((1,), (1,)), ((), ())), preferred_element_type=f32)
    return out[:N], out[N:]


def transform(re, im, table):
    re, im = half_transform(re, im, table)
    return half_transform(re, im, table)


def split_row(row):
    base = pl.multiple_of(jnp.minimum(row // 8 * 8, SIDE - TALL), 8)
    return base, row - base


def spec(space=pltpu.VMEM):
    return pl.BlockSpec(memory_space=space)


def call(kernel, name, ins, outs, scratch=(), flops=0, nbytes=0):
    return pl.pallas_call(
        kernel,
        name=name,
        out_shape=[jax.ShapeDtypeStruct(o, f32) for o in outs],
        in_specs=ins,
        out_specs=[spec() for _ in outs],
        scratch_shapes=list(scratch),
        compiler_params=pltpu.CompilerParams(vmem_limit_bytes=VMEM_LIMIT),
        cost_estimate=pl.CostEstimate(flops=flops, bytes_accessed=nbytes, transcendentals=0),
    )


V = spec()
S = spec(pltpu.SMEM)
MiB = 1 << 20


def first_kernel(where, positions, weight, obj, probe, table, patches, power, total, psi):
    w = weight[0]
    frame = 4 * lax.rem(where[0], 2) + 2 * where[2]
    lit = jnp.zeros((N, N), f32)
    for f in range(2):
        base, down = split_row(positions[frame + f, 0])
        col = positions[frame + f, 1]
        parts = []
        for ch in range(2):
            rows = obj[ch, pl.ds(base, TALL), :]
            part = pltpu.roll(rows, lax.rem(SIDE - col, SIDE), 1)[:, :N]
            part = pltpu.roll(part, lax.rem(TALL - down, TALL), 0)[:N]
            patches[f, ch] = part
            parts.append(part)
        o_re, o_im = parts
        lit = lit + (o_re * o_re + o_im * o_im)
        p_re, p_im = probe[0], probe[1]
        re, im = transform(p_re * o_re - p_im * o_im, p_re * o_im + p_im * o_re, table[...])
        psi[f, 0] = re
        psi[f, 1] = im
        power[f] = w * (re * re + im * im)
    total[...] = lit


def second_kernel(where, weight, patches, probe, power0, a1, a2, a3, b1, b2, b3, table,
                  out0, out1, out2, out3, psi, probes, power):
    zh, c = where[1], where[2]
    power[...] = power0[...]
    wsum = jnp.full((8, N), weight[0], f32)
    flag = jnp.full((1, N), c, jnp.int32) == 0
    for i, (a, b) in enumerate(((a1, b1), (a2, b2), (a3, b3))):
        own, other = a[:N, :], b[:N, :]
        probes[i, 0] = jnp.where(flag, own, other)
        probes[i, 1] = jnp.where(flag, other, own)
        wsum = wsum + a[N:, :]
    for i, a in enumerate((a1, a2, a3)):
        w = a[N:N + 1, :]
        for f in range(2):
            p_re, p_im = probes[i, 0], probes[i, 1]
            o_re, o_im = patches[f, 0], patches[f, 1]
            re, im = transform(p_re * o_re - p_im * o_im, p_re * o_im + p_im * o_re, table[...])
            psi[i, f, 0] = re
            psi[i, f, 1] = im
            power[f] += w * (re * re + im * im)
    for s, out in enumerate((out0, out1, out2, out3)):
        j = lax.rem(zh + s, 4)
        out[:128, :] = power[j // 2, pl.ds(pl.multiple_of((j % 2) * 128, 128), 128), :]
        out[128:136, :] = wsum
        rows = pl.ds(pl.multiple_of(128 * c + 32 * j, 32), 32)
        re, im = probe[0, rows, :], probe[1, rows, :]
        light = re * re + im * im
        for i in range(3):
            re, im = probes[i, 0, rows, :], probes[i, 1, rows, :]
            light = light + (re * re + im * im)
        out[136:168, :] = light


def factor_kernel(m0, m1, m2, m3, measured, out):
    total = (m0[...] + m1[...]) + (m2[...] + m3[...])
    model = total[:128] / total[128:129]
    out[:128, :] = jnp.sqrt(measured[...]) / jnp.sqrt(model + intensity_offset) - 1.0
    out[128:, :] = total[136:]


def third_kernel(where, positions, f0, f1, f2, f3, patches, lit, probe, probes, psi0, psi, table,
                 gkeep, gsend, keep, send, factor, canvas, q):
    y, zh, c = where[0], where[1], where[2]
    frame = 4 * lax.rem(y, 2) + 2 * c
    for s, f in enumerate((f0, f1, f2, f3)):
        factor[lax.rem(zh + 4 - s, 4)] = f[:128, :]
    canvas[...] = jnp.zeros_like(canvas)
    for f in range(2):
        fac = jnp.concatenate([factor[2 * f], factor[2 * f + 1]], axis=0)
        o_re, o_im = patches[f, 0], patches[f, 1]
        g_re = jnp.zeros((N, N), f32)
        g_im = jnp.zeros((N, N), f32)
        for i in range(4):
            a_re, a_im = (psi0[f, 0], psi0[f, 1]) if i == 0 else (psi[i - 1, f, 0], psi[i - 1, f, 1])
            p_re, p_im = (probe[0], probe[1]) if i == 0 else (probes[i - 1, 0], probes[i - 1, 1])
            re, im = transform(a_re * fac, a_im * fac, table[...])
            g_re = g_re + (p_re * re + p_im * im)
            g_im = g_im + (p_re * im - p_im * re)
            q_re = o_re * re + o_im * im
            q_im = o_re * im - o_im * re
            if f == 0:
                q[0, i] = q_re
                q[1, i] = q_im
            else:
                q[0, i] += q_re
                q[1, i] += q_im
        base, down = split_row(positions[frame + f, 0])
        col = positions[frame + f, 1]
        for ch, g in enumerate((g_re, g_im)):
            tall = pltpu.roll(jnp.concatenate([g, jnp.zeros((TALL - N, N), f32)], axis=0), down, 0)
            wide = pltpu.roll(jnp.concatenate([tall, jnp.zeros((TALL, N), f32)], axis=1), col, 1)
            canvas[ch, pl.ds(base, TALL), :] += wide
    for ch in range(2):
        gkeep[ch] = canvas[ch, pl.ds(pl.multiple_of(c * N, N), N), :]
        gsend[ch] = canvas[ch, pl.ds(pl.multiple_of((1 - c) * N, N), N), :]
    for xc in range(4):
        for i in range(4):
            keep[xc, 64 * i:64 * i + 64, :] = q[c, i, 64 * xc:64 * xc + 64, :]
            send[xc, 64 * i:64 * i + 64, :] = q[1 - c, i, 64 * xc:64 * xc + 64, :]
        keep[xc, 256:, :] = lit[64 * xc:64 * xc + 64, :]
        send[xc, 256:, :] = lit[64 * xc:64 * xc + 64, :]


def fold_kernel(where, keep, got, own, out):
    odd = lax.rem(where[0], 2)
    mine = pl.ds(pl.multiple_of(odd * 128, 128), 128)
    theirs = pl.ds(pl.multiple_of((1 - odd) * 128, 128), 128)
    for ch in range(2):
        out[ch] = keep[ch, theirs, :] + got[ch, theirs, :]
        own[ch] = keep[ch, mine, :] + got[ch, mine, :]


def mix_kernel(where, keep, got, o0, o1, o2, o3):
    for s, out in enumerate((o0, o1, o2, o3)):
        j = lax.rem(where[3] + s, 4)
        out[...] = keep[j] + got[j]


def sum_kernel(where, own, got, o0, o1, o2, o3):
    for s, out in enumerate((o0, o1, o2, o3)):
        rows = pl.ds(pl.multiple_of(lax.rem(where[1] + s, 4) * 32, 32), 32)
        for ch in range(2):
            out[ch] = own[ch, rows, :] + got[ch, rows, :]


def rows_kernel(where, f0, f1, f2, f3, out):
    for s, f in enumerate((f0, f1, f2, f3)):
        out[pl.ds(pl.multiple_of(lax.rem(where[1] + 4 - s, 4) * 32, 32), 32), :] = f[128:, :]


def light_kernel(where, positions, near, far, out, padded):
    padded[:32, :] = jnp.zeros((32, N), f32)
    padded[pl.ds(pl.multiple_of(32 + 128 * where[2], 32), 128), :] = near[...]
    padded[pl.ds(pl.multiple_of(32 + 128 * (1 - where[2]), 32), 128), :] = far[...]
    padded[288:328, :] = jnp.zeros((40, N), f32)
    first = 256 * where[2] + 128 * lax.rem(where[0], 2) + 32 * where[1]
    total = jnp.zeros((32, SIDE), f32)
    for f in range(8):
        start = jnp.clip(first - positions[f, 0] + 32, 0, 288)
        base = start // 8 * 8
        rows = padded[pl.ds(pl.multiple_of(base, 8), 40), :]
        rows = pltpu.roll(rows, lax.rem(40 - (start - base), 40), 0)[:32]
        wide = jnp.concatenate([rows, jnp.zeros((32, N), f32)], axis=1)
        total = total + pltpu.roll(wide, positions[f, 1], 1)
    out[...] = total


def update_kernel(o0, o1, o2, o3, obj, light, q0, q1, q2, q3, out, p0, p1, p2, p3):
    scale = light[...] + damping
    for ch in range(2):
        out[ch] = obj[ch] + ((o0[ch] + o1[ch]) + (o2[ch] + o3[ch])) / scale
    power = (q0[256:, :] + q1[256:, :]) + (q2[256:, :] + q3[256:, :])
    for s, p in enumerate((p0, p1, p2, p3)):
        rows = slice(64 * s, 64 * s + 64)
        p[:64, :] = (q0[rows, :] + q1[rows, :]) + (q2[rows, :] + q3[rows, :])
        p[64:, :] = power


def block_kernel(where, n0, n1, n2, n3, q0, q1, q2, q3, out, q):
    for s, n in enumerate((n0, n1, n2, n3)):
        rows = pl.ds(pl.multiple_of(lax.rem(where[1] + 4 - s, 4) * 32, 32), 32)
        for ch in range(2):
            out[ch, rows, :] = n[ch]
    q[...] = (q0[...] + q1[...]) + (q2[...] + q3[...])


def probe_kernel(q0, q1, mine, new):
    new[...] = mine[...] + (q0[:64, :] + q1[:64, :]) / (q0[64:, :] + q1[64:, :] + damping)


def split_kernel(where, b0, b1, b2, b3, n0, n1, n2, n3, keep, send, half):
    y, c, x = where[0], where[2], where[3]
    for s, (b, n) in enumerate(((b0, n0), (b1, n1), (b2, n2), (b3, n3))):
        source = lax.rem(y + 4 - s, 4)
        rows = pl.ds(pl.multiple_of(lax.rem(source, 2) * 128, 128), 128)

        @pl.when(source // 2 == c)
        def _():
            for ch in range(2):
                keep[ch, rows, :] = b[ch]

        @pl.when(source // 2 != c)
        def _():
            for ch in range(2):
                send[ch, rows, :] = b[ch]

        half[pl.ds(pl.multiple_of(lax.rem(x + 4 - s, 4) * 64, 64), 64), :] = n[...]


def last_kernel(where, keep, got, half, other, tile, probe):
    c = where[2]
    for ch in range(2):
        tile[ch, pl.ds(pl.multiple_of(c * N, N), N), :] = keep[ch]
        tile[ch, pl.ds(pl.multiple_of((1 - c) * N, N), N), :] = got[ch]
    probe[c] = half[...]
    probe[1 - c] = other[...]


def shift(x, axis, n, s):
    return lax.ppermute(x, axis, [(i, (i + s) % n) for i in range(n)])


def local(object_field, probes, measured, positions, weights):
    forward, inverse = (jnp.asarray(t) for t in tables())
    y, zh, c, x = (lax.axis_index(a) for a in ("y", "zh", "c", "x"))
    where = jnp.stack([y, zh, c, x]).astype(jnp.int32)
    probe = probes[0]
    steps = (1, 2, 3)

    def ring(parts, axis, sign=1):
        return [parts[0]] + [shift(parts[s], axis, 4, sign * s) for s in steps]

    def swap(value):
        return shift(value, "c", 2, 1)

    def small(kernel, name, ins, outs, *operands):
        return call(kernel, name, ins, outs, flops=10**6, nbytes=MiB)(*operands)

    own = lax.dynamic_index_in_dim(probe, c, 0, False)
    message = jnp.concatenate([own, jnp.broadcast_to(weights[:, None], (8, N))], axis=0)
    near = ring([message] * 4, "y")[1:]

    mine = y // 2 == c
    offsets = jnp.where(mine, positions[0, 0], swap(positions[0, 0]))
    tile = jnp.where(mine, object_field, swap(object_field))
    halves = measured.reshape(16, 128, N)
    place = 8 * (y % 2) + zh
    taken = [lax.dynamic_index_in_dim(halves, place + 4 * i, 0, False) for i in (c, 1 - c)]
    intensity = jnp.where(mine, taken[0], swap(taken[1]))

    plane = (N, N)
    patches, power0, lit, psi0 = call(
        first_kernel, "first", [S, S, S, V, V, V],
        [(2, 2) + plane, (2,) + plane, plane, (2, 2) + plane], flops=5 * 10**9, nbytes=6 * MiB,
    )(where, offsets, weights, tile, probe, forward)

    near = [lax.optimization_barrier((m, power0))[0] for m in near]
    far = [swap(m) for m in near]
    *sums, psi, others = call(
        second_kernel, "second", [S, S] + [V] * 10,
        [(168, N)] * 4 + [(3, 2, 2) + plane, (3, 2) + plane],
        [pltpu.VMEM((2,) + plane, f32)], flops=15 * 10**9, nbytes=10 * MiB,
    )(where, weights, patches, probe, power0, *near, *far, forward)

    (factor,) = small(factor_kernel, "factor", [V] * 5, [(160, N)], *ring(sums, "zh"), intensity)
    factors = ring([factor] * 4, "zh")

    gkeep, gsend, keep, send = call(
        third_kernel, "third", [S, S] + [V] * 11,
        [(2, N, SIDE)] * 2 + [(4, 320, N)] * 2,
        [pltpu.VMEM((4, 128, N), f32), pltpu.VMEM((2, SIDE, SIDE), f32), pltpu.VMEM((2, 4) + plane, f32)],
        flops=20 * 10**9, nbytes=14 * MiB,
    )(where, offsets, *factors, patches, lit, probe, others, psi0, psi, inverse)

    quarter, part = (2, 128, SIDE), (2, 32, SIDE)
    own, out = small(fold_kernel, "fold", [S, V, V], [quarter] * 2, where, gkeep, swap(gsend))
    got = lax.ppermute(out, "y", [(0, 1), (1, 0), (2, 3), (3, 2)])
    mixed = ring(small(mix_kernel, "mix", [S, V, V], [(320, N)] * 4, where, keep, swap(send)), "x")

    (rows,) = small(rows_kernel, "rows", [S] + [V] * 4, [(128, N)], where, *factors)
    (light,) = call(
        light_kernel, "light", [S, S, V, V], [(32, SIDE)], [pltpu.VMEM((328, N), f32)],
        flops=10**6, nbytes=MiB,
    )(where, offsets, rows, swap(rows))
    target = lax.dynamic_index_in_dim(tile.reshape(2, 16, 32, SIDE), 8 * c + 4 * (y % 2) + zh, 1, False)
    own_rows = lax.dynamic_slice(probe, (c, 64 * x, 0), (1, 64, N))[0]

    sums = ring(small(sum_kernel, "sum", [S, V, V], [part] * 4, where, own, got), "zh")
    new, *qs = small(
        update_kernel, "update", [V] * 10, [part] + [(128, N)] * 4, *sums, target, light, *mixed
    )
    new = ring([new] * 4, "zh")
    qs = ring(qs, "y", -1)
    block, q = small(block_kernel, "block", [S] + [V] * 8, [quarter, (128, N)], where, *new, *qs)
    blocks = ring([block] * 4, "y")
    (chunk,) = small(probe_kernel, "probe", [V] * 3, [(64, N)], q, shift(q, "zl", 2, 1), own_rows)
    chunks = ring([chunk] * 4, "x")
    keep, send, half = small(
        split_kernel, "split", [S] + [V] * 8, [(2, N, SIDE)] * 2 + [plane], where, *blocks, *chunks
    )
    new_object, new_probe = small(
        last_kernel, "last", [S] + [V] * 4, [(2, SIDE, SIDE), (2,) + plane],
        where, keep, swap(send), half, swap(half),
    )
    return new_object, new_probe[None]


def solution(mesh):
    inner = Mesh(mesh.devices.reshape(4, 4, 2, 2, 4), ("y", "zh", "zl", "c", "x"))
    wave, ty, tx = ("y", "zh"), ("zl", "c"), "x"
    in_specs = (
        P(None, ty, tx),
        P(wave, None, None, None),
        P(ty, tx, None, None, None),
        P(ty, tx, None, None),
        P(wave),
    )
    out_specs = (P(None, ty, tx), P(wave, None, None, None))
    return jax.shard_map(local, mesh=inner, in_specs=in_specs, out_specs=out_specs, check_vma=False)
```

```python
import math

import jax
import jax.numpy as jnp
import ml_dtypes
import numpy as np
from jax import lax
from jax.experimental import pallas as pl
from jax.experimental.pallas import tpu as pltpu
from jax.sharding import Mesh
from jax.sharding import PartitionSpec as P

f32 = jnp.float32
bf16 = jnp.bfloat16
damping = 1.0
intensity_offset = 0.1
N = 256
H = 128
SIDE = 512
TALL = 264


def tables():
    k = np.arange(H)
    angle = 2.0 * math.pi / H * (np.outer(k, k) % H)
    c, s = np.cos(angle) / 16.0, -np.sin(angle) / 16.0
    forward, inverse = np.block([[c, -s], [s, c]]), np.block([[c, s], [-s, c]])

    def split(table, axis):
        high = table.astype(np.float32).astype(ml_dtypes.bfloat16)
        low = (table - high.astype(np.float64)).astype(np.float32).astype(ml_dtypes.bfloat16)
        return np.concatenate([high, high, low], axis=axis)

    turn = np.exp(-2j * math.pi * k / N)
    turn = np.stack([turn.real, turn.imag]).astype(np.float32)
    rows = np.broadcast_to(turn[:, :, None], (2, H, H)).copy()
    return [split(t.T, 0) for t in (forward, inverse)], [split(t, 1) for t in (forward, inverse)], turn, rows


def split_data(x, axis):
    high = x.astype(bf16)
    low = (x - high.astype(f32)).astype(bf16)
    return jnp.concatenate([high, low, high], axis=axis)


def cat(parts, axis):
    return jnp.concatenate(parts, axis=axis)


def twiddle(re, im, wr, wi):
    return re * wr - im * wi, re * wi + im * wr


def transform(re, im, right, left, turn, rows):
    a, b, ai, bi = re[:, :H], re[:, H:], im[:, :H], im[:, H:]
    o_re, o_im = twiddle(a - b, ai - bi, turn[0:1, :], turn[1:2, :])
    x = cat([cat([a + b, ai + bi], 1), cat([o_re, o_im], 1)], 0)
    x = jnp.dot(split_data(x, 1), right[...], preferred_element_type=f32)
    re, im = cat([x[:N, :H], x[N:, :H]], 1), cat([x[:N, H:], x[N:, H:]], 1)
    a, b, ai, bi = re[:H], re[H:], im[:H], im[H:]
    wr, wi = cat([rows[0]] * 2, 1), cat([rows[1]] * 2, 1)
    o_re, o_im = twiddle(a - b, ai - bi, wr, wi)
    x = cat([cat([a + b, ai + bi], 0), cat([o_re, o_im], 0)], 1)
    x = jnp.dot(left[...], split_data(x, 0), preferred_element_type=f32)
    return cat([x[:H, :N], x[:H, N:]], 0), cat([x[H:, :N], x[H:, N:]], 0)


def restore(re, im, right, left, turn, rows):
    x = cat([cat([re[:, :H], im[:, :H]], 1), cat([re[:, H:], im[:, H:]], 1)], 0)
    x = jnp.dot(split_data(x, 1), right[...], preferred_element_type=f32)
    o_re, o_im = twiddle(x[N:, :H], x[N:, H:], turn[0:1, :], -turn[1:2, :])
    e_re, e_im = x[:N, :H], x[:N, H:]
    re, im = cat([e_re + o_re, e_re - o_re], 1), cat([e_im + o_im, e_im - o_im], 1)
    x = cat([cat([re[:H], im[:H]], 0), cat([re[H:], im[H:]], 0)], 1)
    x = jnp.dot(left[...], split_data(x, 0), preferred_element_type=f32)
    wr, wi = cat([rows[0]] * 2, 1), -cat([rows[1]] * 2, 1)
    o_re, o_im = twiddle(x[:H, N:], x[H:, N:], wr, wi)
    e_re, e_im = x[:H, :N], x[H:, :N]
    return cat([e_re + o_re, e_re - o_re], 0), cat([e_im + o_im, e_im - o_im], 0)


def split_row(row):
    base = pl.multiple_of(jnp.minimum(row // 8 * 8, SIDE - TALL), 8)
    return base, row - base


def spec(space=pltpu.VMEM):
    return pl.BlockSpec(memory_space=space)


def call(kernel, name, ins, outs, scratch=(), flops=0, nbytes=0, limit=16):
    return pl.pallas_call(
        kernel,
        name=name,
        out_shape=[jax.ShapeDtypeStruct(o, f32) for o in outs],
        in_specs=ins,
        out_specs=[spec() for _ in outs],
        scratch_shapes=list(scratch),
        compiler_params=pltpu.CompilerParams(vmem_limit_bytes=limit * MiB),
        cost_estimate=pl.CostEstimate(flops=flops, bytes_accessed=nbytes, transcendentals=0),
    )


V = spec()
S = spec(pltpu.SMEM)
MiB = 1 << 20


def first_kernel(where, positions, weight, obj, probe, right, left, turn, rows128,
                 patches, power, total, psi):
    table = (right, left, turn, rows128)
    w = weight[0]
    frame = 4 * lax.rem(where[0], 2) + 2 * where[2]
    lit = jnp.zeros((N, N), f32)
    for f in range(2):
        base, down = split_row(positions[frame + f, 0])
        col = positions[frame + f, 1]
        parts = []
        for ch in range(2):
            rows = obj[ch, pl.ds(base, TALL), :]
            part = pltpu.roll(rows, lax.rem(SIDE - col, SIDE), 1)[:, :N]
            part = pltpu.roll(part, lax.rem(TALL - down, TALL), 0)[:N]
            patches[f, ch] = part
            parts.append(part)
        o_re, o_im = parts
        lit = lit + (o_re * o_re + o_im * o_im)
        p_re, p_im = probe[0], probe[1]
        re, im = transform(p_re * o_re - p_im * o_im, p_re * o_im + p_im * o_re, *table)
        psi[f, 0] = re
        psi[f, 1] = im
        power[f] = w * (re * re + im * im)
    total[...] = lit


def second_kernel(where, weight, patches, probe, power0, a1, a2, a3, b1, b2, b3, right, left, turn, rows128,
                  out0, out1, out2, out3, psi, probes, power):
    table = (right, left, turn, rows128)
    zh, c = where[1], where[2]
    power[...] = power0[...]
    wsum = jnp.full((8, N), weight[0], f32)
    flag = jnp.full((1, N), c, jnp.int32) == 0
    for i, (a, b) in enumerate(((a1, b1), (a2, b2), (a3, b3))):
        own, other = a[:N, :], b[:N, :]
        probes[i, 0] = jnp.where(flag, own, other)
        probes[i, 1] = jnp.where(flag, other, own)
        wsum = wsum + a[N:, :]
    for i, a in enumerate((a1, a2, a3)):
        w = a[N:N + 1, :]
        for f in range(2):
            p_re, p_im = probes[i, 0], probes[i, 1]
            o_re, o_im = patches[f, 0], patches[f, 1]
            re, im = transform(p_re * o_re - p_im * o_im, p_re * o_im + p_im * o_re, *table)
            psi[i, f, 0] = re
            psi[i, f, 1] = im
            power[f] += w * (re * re + im * im)
    for s, out in enumerate((out0, out1, out2, out3)):
        j = lax.rem(zh + s, 4)
        out[:128, :] = power[j // 2, pl.ds(pl.multiple_of((j % 2) * 128, 128), 128), :]
        out[128:136, :] = wsum
        rows = pl.ds(pl.multiple_of(128 * c + 32 * j, 32), 32)
        re, im = probe[0, rows, :], probe[1, rows, :]
        light = re * re + im * im
        for i in range(3):
            re, im = probes[i, 0, rows, :], probes[i, 1, rows, :]
            light = light + (re * re + im * im)
        out[136:168, :] = light


def order_kernel(where, frame, out):
    parity = lax.rem(where[1], 2)
    i, r = lax.broadcasted_iota(jnp.int32, (H, N), 0), lax.broadcasted_iota(jnp.int32, (H, N), 1)
    pick_rows = jnp.where(r == 2 * i + parity, 1.0, 0.0).astype(bf16)
    r, j = lax.broadcasted_iota(jnp.int32, (N, N), 0), lax.broadcasted_iota(jnp.int32, (N, N), 1)
    pick_columns = jnp.where(r == jnp.where(j < H, 2 * j, 2 * j - (N - 1)), 1.0, 0.0).astype(bf16)
    rest = frame[...]
    total = jnp.zeros((H, N), f32)
    for _ in range(3):
        part = rest.astype(bf16)
        rest = rest - part.astype(f32)
        part = jnp.dot(pick_rows, part, preferred_element_type=f32).astype(bf16)
        total = total + jnp.dot(part, pick_columns, preferred_element_type=f32)
    out[...] = total


def factor_kernel(m0, m1, m2, m3, measured, out):
    total = (m0[...] + m1[...]) + (m2[...] + m3[...])
    model = total[:128] / total[128:129]
    out[:128, :] = jnp.sqrt(measured[...]) / jnp.sqrt(model + intensity_offset) - 1.0
    out[128:, :] = total[136:]


def third_kernel(where, positions, f0, f1, f2, f3, patches, lit, probe, probes, psi0, psi, right, left, turn, rows128,
                 gkeep, gsend, keep, send, factor, canvas, q):
    table = (right, left, turn, rows128)
    y, zh, c = where[0], where[1], where[2]
    frame = 4 * lax.rem(y, 2) + 2 * c
    for s, f in enumerate((f0, f1, f2, f3)):
        factor[lax.rem(zh + 4 - s, 4)] = f[:128, :]
    canvas[...] = jnp.zeros_like(canvas)
    for f in range(2):
        fac = jnp.concatenate([factor[2 * f], factor[2 * f + 1]], axis=0)
        o_re, o_im = patches[f, 0], patches[f, 1]
        g_re = jnp.zeros((N, N), f32)
        g_im = jnp.zeros((N, N), f32)
        for i in range(4):
            a_re, a_im = (psi0[f, 0], psi0[f, 1]) if i == 0 else (psi[i - 1, f, 0], psi[i - 1, f, 1])
            p_re, p_im = (probe[0], probe[1]) if i == 0 else (probes[i - 1, 0], probes[i - 1, 1])
            re, im = restore(a_re * fac, a_im * fac, *table)
            g_re = g_re + (p_re * re + p_im * im)
            g_im = g_im + (p_re * im - p_im * re)
            q_re = o_re * re + o_im * im
            q_im = o_re * im - o_im * re
            if f == 0:
                q[0, i] = q_re
                q[1, i] = q_im
            else:
                q[0, i] += q_re
                q[1, i] += q_im
        base, down = split_row(positions[frame + f, 0])
        col = positions[frame + f, 1]
        for ch, g in enumerate((g_re, g_im)):
            tall = pltpu.roll(jnp.concatenate([g, jnp.zeros((TALL - N, N), f32)], axis=0), down, 0)
            wide = pltpu.roll(jnp.concatenate([tall, jnp.zeros((TALL, N), f32)], axis=1), col, 1)
            canvas[ch, pl.ds(base, TALL), :] += wide
    for ch in range(2):
        gkeep[ch] = canvas[ch, pl.ds(pl.multiple_of(c * N, N), N), :]
        gsend[ch] = canvas[ch, pl.ds(pl.multiple_of((1 - c) * N, N), N), :]
    for xc in range(4):
        for i in range(4):
            keep[xc, 64 * i:64 * i + 64, :] = q[c, i, 64 * xc:64 * xc + 64, :]
            send[xc, 64 * i:64 * i + 64, :] = q[1 - c, i, 64 * xc:64 * xc + 64, :]
        keep[xc, 256:, :] = lit[64 * xc:64 * xc + 64, :]
        send[xc, 256:, :] = lit[64 * xc:64 * xc + 64, :]


def fold_kernel(where, keep, got, own, out):
    odd = lax.rem(where[0], 2)
    mine = pl.ds(pl.multiple_of(odd * 128, 128), 128)
    theirs = pl.ds(pl.multiple_of((1 - odd) * 128, 128), 128)
    for ch in range(2):
        out[ch] = keep[ch, theirs, :] + got[ch, theirs, :]
        own[ch] = keep[ch, mine, :] + got[ch, mine, :]


def mix_kernel(where, keep, got, o0, o1, o2, o3):
    for s, out in enumerate((o0, o1, o2, o3)):
        j = lax.rem(where[3] + s, 4)
        out[...] = keep[j] + got[j]


def sum_kernel(where, own, got, o0, o1, o2, o3):
    for s, out in enumerate((o0, o1, o2, o3)):
        rows = pl.ds(pl.multiple_of(lax.rem(where[1] + s, 4) * 32, 32), 32)
        for ch in range(2):
            out[ch] = own[ch, rows, :] + got[ch, rows, :]


def rows_kernel(where, f0, f1, f2, f3, out):
    for s, f in enumerate((f0, f1, f2, f3)):
        out[pl.ds(pl.multiple_of(lax.rem(where[1] + 4 - s, 4) * 32, 32), 32), :] = f[128:, :]


def light_kernel(where, positions, near, far, out, padded):
    padded[:32, :] = jnp.zeros((32, N), f32)
    padded[pl.ds(pl.multiple_of(32 + 128 * where[2], 32), 128), :] = near[...]
    padded[pl.ds(pl.multiple_of(32 + 128 * (1 - where[2]), 32), 128), :] = far[...]
    padded[288:328, :] = jnp.zeros((40, N), f32)
    first = 256 * where[2] + 128 * lax.rem(where[0], 2) + 32 * where[1]
    total = jnp.zeros((32, SIDE), f32)
    for f in range(8):
        start = jnp.clip(first - positions[f, 0] + 32, 0, 288)
        base = start // 8 * 8
        rows = padded[pl.ds(pl.multiple_of(base, 8), 40), :]
        rows = pltpu.roll(rows, lax.rem(40 - (start - base), 40), 0)[:32]
        wide = jnp.concatenate([rows, jnp.zeros((32, N), f32)], axis=1)
        total = total + pltpu.roll(wide, positions[f, 1], 1)
    out[...] = total


def probe_sum_kernel(q0, q1, q2, q3, p0, p1, p2, p3):
    power = (q0[256:, :] + q1[256:, :]) + (q2[256:, :] + q3[256:, :])
    for s, p in enumerate((p0, p1, p2, p3)):
        rows = slice(64 * s, 64 * s + 64)
        p[:64, :] = (q0[rows, :] + q1[rows, :]) + (q2[rows, :] + q3[rows, :])
        p[64:, :] = power


def update_kernel(o0, o1, o2, o3, obj, light, q0, q1, q2, q3, out, q):
    scale = light[...] + damping
    for ch in range(2):
        out[ch] = obj[ch] + ((o0[ch] + o1[ch]) + (o2[ch] + o3[ch])) / scale
    q[...] = (q0[...] + q1[...]) + (q2[...] + q3[...])


def block_kernel(where, n0, n1, n2, n3, q0, q1, mine, out, new):
    for s, n in enumerate((n0, n1, n2, n3)):
        rows = pl.ds(pl.multiple_of(lax.rem(where[1] + 4 - s, 4) * 32, 32), 32)
        for ch in range(2):
            out[ch, rows, :] = n[ch]
    new[...] = mine[...] + (q0[:64, :] + q1[:64, :]) / (q0[64:, :] + q1[64:, :] + damping)


def split_kernel(where, b0, b1, b2, b3, n0, n1, n2, n3, keep, send, half):
    y, c, x = where[0], where[2], where[3]
    for s, (b, n) in enumerate(((b0, n0), (b1, n1), (b2, n2), (b3, n3))):
        source = lax.rem(y + 4 - s, 4)
        rows = pl.ds(pl.multiple_of(lax.rem(source, 2) * 128, 128), 128)

        @pl.when(source // 2 == c)
        def _():
            for ch in range(2):
                keep[ch, rows, :] = b[ch]

        @pl.when(source // 2 != c)
        def _():
            for ch in range(2):
                send[ch, rows, :] = b[ch]

        half[pl.ds(pl.multiple_of(lax.rem(x + 4 - s, 4) * 64, 64), 64), :] = n[...]


def last_kernel(where, keep, got, half, other, tile, probe):
    c = where[2]
    for ch in range(2):
        tile[ch, pl.ds(pl.multiple_of(c * N, N), N), :] = keep[ch]
        tile[ch, pl.ds(pl.multiple_of((1 - c) * N, N), N), :] = got[ch]
    probe[c] = half[...]
    probe[1 - c] = other[...]


def shift(x, axis, n, s):
    return lax.ppermute(x, axis, [(i, (i + s) % n) for i in range(n)])


def local(object_field, probes, measured, positions, weights):
    rights, lefts, turn, turn_rows = tables()
    forward, inverse = (
        tuple(jnp.asarray(t) for t in (rights[i], lefts[i], turn, turn_rows)) for i in range(2)
    )
    y, zh, c, x = (lax.axis_index(a) for a in ("y", "zh", "c", "x"))
    where = jnp.stack([y, zh, c, x]).astype(jnp.int32)
    probe = probes[0]
    steps = (1, 2, 3)

    def ring(parts, axis, sign=1):
        return [parts[0]] + [shift(parts[s], axis, 4, sign * s) for s in steps]

    def swap(value):
        return shift(value, "c", 2, 1)

    def small(kernel, name, ins, outs, *operands):
        return call(kernel, name, ins, outs, flops=10**6, nbytes=MiB)(*operands)

    own = lax.dynamic_index_in_dim(probe, c, 0, False)
    message = jnp.concatenate([own, jnp.broadcast_to(weights[:, None], (8, N))], axis=0)
    near = ring([message] * 4, "y")[1:]

    mine = y // 2 == c
    offsets = jnp.where(mine, positions[0, 0], swap(positions[0, 0]))
    tile = jnp.where(mine, object_field, swap(object_field))
    place = 4 * (y % 2) + zh // 2
    taken = [lax.dynamic_index_in_dim(measured[0, 0], place + 2 * i, 0, False) for i in (c, 1 - c)]
    intensity = jnp.where(mine, taken[0], swap(taken[1]))
    (intensity,) = small(order_kernel, "order", [S, V], [(H, N)], where, intensity)

    plane = (N, N)
    patches, power0, lit, psi0 = call(
        first_kernel, "first", [S, S, S] + [V] * 6,
        [(2, 2) + plane, (2,) + plane, plane, (2, 2) + plane], flops=5 * 10**9, nbytes=6 * MiB,
    )(where, offsets, weights, tile, probe, *forward)

    near = [lax.optimization_barrier((m, power0))[0] for m in near]
    far = [swap(m) for m in near]
    *sums, psi, others = call(
        second_kernel, "second", [S, S] + [V] * 13,
        [(168, N)] * 4 + [(3, 2, 2) + plane, (3, 2) + plane],
        [pltpu.VMEM((2,) + plane, f32)], flops=15 * 10**9, nbytes=10 * MiB, limit=24,
    )(where, weights, patches, probe, power0, *near, *far, *forward)

    (factor,) = small(factor_kernel, "factor", [V] * 5, [(160, N)], *ring(sums, "zh"), intensity)
    factors = ring([factor] * 4, "zh")

    gkeep, gsend, keep, send = call(
        third_kernel, "third", [S, S] + [V] * 14,
        [(2, N, SIDE)] * 2 + [(4, 320, N)] * 2,
        [pltpu.VMEM((4, 128, N), f32), pltpu.VMEM((2, SIDE, SIDE), f32), pltpu.VMEM((2, 4) + plane, f32)],
        flops=20 * 10**9, nbytes=14 * MiB, limit=36,
    )(where, offsets, *factors, patches, lit, probe, others, psi0, psi, *inverse)

    quarter, part = (2, 128, SIDE), (2, 32, SIDE)
    own, out = small(fold_kernel, "fold", [S, V, V], [quarter] * 2, where, gkeep, swap(gsend))
    got = lax.ppermute(out, "y", [(0, 1), (1, 0), (2, 3), (3, 2)])
    mixed = ring(small(mix_kernel, "mix", [S, V, V], [(320, N)] * 4, where, keep, swap(send)), "x")

    (rows,) = small(rows_kernel, "rows", [S] + [V] * 4, [(128, N)], where, *factors)
    (light,) = call(
        light_kernel, "light", [S, S, V, V], [(32, SIDE)], [pltpu.VMEM((328, N), f32)],
        flops=10**6, nbytes=MiB,
    )(where, offsets, rows, swap(rows))
    target = lax.dynamic_index_in_dim(tile.reshape(2, 16, 32, SIDE), 8 * c + 4 * (y % 2) + zh, 1, False)
    own_rows = lax.dynamic_slice(probe, (c, 64 * x, 0), (1, 64, N))[0]

    sums = ring(small(sum_kernel, "sum", [S, V, V], [part] * 4, where, own, got), "zh")
    qs = ring(small(probe_sum_kernel, "probe_sum", [V] * 4, [(128, N)] * 4, *mixed), "y", -1)
    new, q = small(update_kernel, "update", [V] * 10, [part, (128, N)], *sums, target, light, *qs)
    new = ring([new] * 4, "zh")
    block, chunk = small(
        block_kernel, "block", [S] + [V] * 7, [quarter, (64, N)],
        where, *new, q, shift(q, "zl", 2, 1), own_rows,
    )
    blocks = ring([block] * 4, "y")
    chunks = ring([chunk] * 4, "x")
    keep, send, half = small(
        split_kernel, "split", [S] + [V] * 8, [(2, N, SIDE)] * 2 + [plane], where, *blocks, *chunks
    )
    new_object, new_probe = small(
        last_kernel, "last", [S] + [V] * 4, [(2, SIDE, SIDE), (2,) + plane],
        where, keep, swap(send), half, swap(half),
    )
    return new_object, new_probe[None]


def solution(mesh):
    inner = Mesh(mesh.devices.reshape(4, 4, 2, 2, 4), ("y", "zh", "zl", "c", "x"))
    wave, ty, tx = ("y", "zh"), ("zl", "c"), "x"
    in_specs = (
        P(None, ty, tx),
        P(wave, None, None, None),
        P(ty, tx, None, None, None),
        P(ty, tx, None, None),
        P(wave),
    )
    out_specs = (P(None, ty, tx), P(wave, None, None, None))
    return jax.shard_map(local, mesh=inner, in_specs=in_specs, out_specs=out_specs, check_vma=False)
```

```python
import math

import jax
import jax.numpy as jnp
import ml_dtypes
import numpy as np
from jax import lax
from jax.experimental import pallas as pl
from jax.experimental.pallas import tpu as pltpu
from jax.sharding import Mesh
from jax.sharding import PartitionSpec as P

f32 = jnp.float32
bf16 = jnp.bfloat16
damping = 1.0
intensity_offset = 0.1
N = 256
H = 128
SIDE = 512
TALL = 264


def tables():
    k = np.arange(H)
    angle = 2.0 * math.pi / H * (np.outer(k, k) % H)
    c, s = np.cos(angle) / 16.0, -np.sin(angle) / 16.0
    forward, inverse = np.block([[c, -s], [s, c]]), np.block([[c, s], [-s, c]])

    def split(table, axis):
        high = table.astype(np.float32).astype(ml_dtypes.bfloat16)
        low = (table - high.astype(np.float64)).astype(np.float32).astype(ml_dtypes.bfloat16)
        return np.concatenate([high, high, low], axis=axis)

    turn = np.exp(-2j * math.pi * k / N)
    turn = np.stack([turn.real, turn.imag]).astype(np.float32)
    rows = np.broadcast_to(turn[:, :, None], (2, H, H)).copy()
    return [split(t.T, 0) for t in (forward, inverse)], [split(t, 1) for t in (forward, inverse)], turn, rows


def split_data(x, axis):
    high = x.astype(bf16)
    low = (x - high.astype(f32)).astype(bf16)
    return jnp.concatenate([high, low, high], axis=axis)


def cat(parts, axis):
    return jnp.concatenate(parts, axis=axis)


def twiddle(re, im, wr, wi):
    return re * wr - im * wi, re * wi + im * wr


def transform(re, im, right, left, turn, rows):
    a, b, ai, bi = re[:, :H], re[:, H:], im[:, :H], im[:, H:]
    o_re, o_im = twiddle(a - b, ai - bi, turn[0:1, :], turn[1:2, :])
    x = cat([cat([a + b, ai + bi], 1), cat([o_re, o_im], 1)], 0)
    x = jnp.dot(split_data(x, 1), right[...], preferred_element_type=f32)
    re, im = cat([x[:N, :H], x[N:, :H]], 1), cat([x[:N, H:], x[N:, H:]], 1)
    a, b, ai, bi = re[:H], re[H:], im[:H], im[H:]
    wr, wi = cat([rows[0]] * 2, 1), cat([rows[1]] * 2, 1)
    o_re, o_im = twiddle(a - b, ai - bi, wr, wi)
    x = cat([cat([a + b, ai + bi], 0), cat([o_re, o_im], 0)], 1)
    x = jnp.dot(left[...], split_data(x, 0), preferred_element_type=f32)
    return cat([x[:H, :N], x[:H, N:]], 0), cat([x[H:, :N], x[H:, N:]], 0)


def restore(re, im, right, left, turn, rows):
    x = cat([cat([re[:, :H], im[:, :H]], 1), cat([re[:, H:], im[:, H:]], 1)], 0)
    x = jnp.dot(split_data(x, 1), right[...], preferred_element_type=f32)
    o_re, o_im = twiddle(x[N:, :H], x[N:, H:], turn[0:1, :], -turn[1:2, :])
    e_re, e_im = x[:N, :H], x[:N, H:]
    re, im = cat([e_re + o_re, e_re - o_re], 1), cat([e_im + o_im, e_im - o_im], 1)
    x = cat([cat([re[:H], im[:H]], 0), cat([re[H:], im[H:]], 0)], 1)
    x = jnp.dot(left[...], split_data(x, 0), preferred_element_type=f32)
    wr, wi = cat([rows[0]] * 2, 1), -cat([rows[1]] * 2, 1)
    o_re, o_im = twiddle(x[:H, N:], x[H:, N:], wr, wi)
    e_re, e_im = x[:H, :N], x[H:, :N]
    return cat([e_re + o_re, e_re - o_re], 0), cat([e_im + o_im, e_im - o_im], 0)


def split_row(row):
    base = pl.multiple_of(jnp.minimum(row // 8 * 8, SIDE - TALL), 8)
    return base, row - base


def spec(space=pltpu.VMEM):
    return pl.BlockSpec(memory_space=space)


def call(kernel, name, ins, outs, scratch=(), flops=0, nbytes=0, limit=16):
    return pl.pallas_call(
        kernel,
        name=name,
        out_shape=[jax.ShapeDtypeStruct(o, f32) for o in outs],
        in_specs=ins,
        out_specs=[spec() for _ in outs],
        scratch_shapes=list(scratch),
        compiler_params=pltpu.CompilerParams(vmem_limit_bytes=limit * MiB),
        cost_estimate=pl.CostEstimate(flops=flops, bytes_accessed=nbytes, transcendentals=0),
    )


V = spec()
S = spec(pltpu.SMEM)
MiB = 1 << 20


def pick(frame, parity):
    i, r = lax.broadcasted_iota(jnp.int32, (H, N), 0), lax.broadcasted_iota(jnp.int32, (H, N), 1)
    pick_rows = jnp.where(r == 2 * i + parity, 1.0, 0.0).astype(bf16)
    r, j = lax.broadcasted_iota(jnp.int32, (N, N), 0), lax.broadcasted_iota(jnp.int32, (N, N), 1)
    pick_columns = jnp.where(r == jnp.where(j < H, 2 * j, 2 * j - (N - 1)), 1.0, 0.0).astype(bf16)
    rest = frame
    total = jnp.zeros((H, N), f32)
    for _ in range(3):
        part = rest.astype(bf16)
        rest = rest - part.astype(f32)
        part = jnp.dot(pick_rows, part, preferred_element_type=f32).astype(bf16)
        total = total + jnp.dot(part, pick_columns, preferred_element_type=f32)
    return total


def first_kernel(where, positions, own_positions, weight, obj, got, frame, got_frame, probe, right, left, turn, rows128,
                 patches, power, total, psi, intensity, squares):
    table = (right, left, turn, rows128)
    y, zh, c = where[0], where[1], where[2]
    mine = zh // 2 == c
    w = weight[0]
    first = 4 * lax.rem(zh, 2) + 2 * c

    def window(source, row, col):
        base, down = split_row(row)
        part = pltpu.roll(source[pl.ds(base, TALL), :], lax.rem(SIDE - col, SIDE), 1)[:, :N]
        return pltpu.roll(part, lax.rem(TALL - down, TALL), 0)[:N]

    def take(source):
        for f in range(2):
            for ch in range(2):
                patches[f, ch] = window(source.at[ch], positions[first + f, 0], positions[first + f, 1])

    @pl.when(mine)
    def _():
        take(obj)

    @pl.when(jnp.logical_not(mine))
    def _():
        take(got)

    for f in range(2):
        o_re, o_im = patches[f, 0], patches[f, 1]
        p_re, p_im = probe[0], probe[1]
        re, im = transform(p_re * o_re - p_im * o_im, p_re * o_im + p_im * o_re, *table)
        psi[f, 0] = re
        psi[f, 1] = im
        power[f] = w * (re * re + im * im)
    squares[...] = obj[0] * obj[0] + obj[1] * obj[1]
    lit = jnp.zeros((N, N), f32)
    for f in range(8):
        lit = lit + window(squares, own_positions[f, 0], own_positions[f, 1])
    total[...] = lit
    flag = jnp.full((1, N), zh // 2 - c, jnp.int32) == 0
    intensity[...] = pick(jnp.where(flag, frame[...], got_frame[...]), lax.rem(y, 2))


def more_waves(where, patches, arrivals, table, power, psi, probes):
    c = where[2]
    flag = jnp.full((1, N), c, jnp.int32) == 0
    mine = pl.ds(pl.multiple_of(128 * c, 128), 128)
    wsum = jnp.zeros((8, N), f32)
    light = jnp.zeros((128, N), f32)
    for i, (a, b) in enumerate(arrivals):
        own, other = a[:N, :], b[:N, :]
        p_re, p_im = jnp.where(flag, own, other), jnp.where(flag, other, own)
        probes[i, 0] = p_re
        probes[i, 1] = p_im
        wsum = wsum + a[N:, :]
        w = a[N:N + 1, :]
        for f in range(2):
            o_re, o_im = patches[f, 0], patches[f, 1]
            re, im = transform(p_re * o_re - p_im * o_im, p_re * o_im + p_im * o_re, *table)
            psi[i, f, 0] = re
            psi[i, f, 1] = im
            power[f] += w * (re * re + im * im)
        re, im = probes[i, 0, mine, :], probes[i, 1, mine, :]
        light = light + (re * re + im * im)
    return wsum, light


def second_kernel(where, weight, patches, probe, power0, a1, a2, a3, b1, b2, b3, right, left, turn, rows128,
                  out0, out1, out2, out3, psi, probes, power, lights):
    power[...] = power0[...]
    wsum, light = more_waves(
        where, patches, ((a1, b1), (a2, b2), (a3, b3)), (right, left, turn, rows128), power, psi, probes
    )
    wsum = wsum + weight[0]
    mine = pl.ds(pl.multiple_of(128 * where[2], 128), 128)
    re, im = probe[0, mine, :], probe[1, mine, :]
    lights[...] = light + (re * re + im * im)
    for s, out in enumerate((out0, out1, out2, out3)):
        j = lax.rem(where[0] + s, 4)
        out[:128, :] = power[j // 2, pl.ds(pl.multiple_of((j % 2) * 128, 128), 128), :]
        out[128:136, :] = wsum
        out[136:168, :] = lights[pl.ds(pl.multiple_of(32 * j, 32), 32), :]


def factor_kernel(m0, m1, m2, m3, measured, out):
    total = (m0[...] + m1[...]) + (m2[...] + m3[...])
    model = total[:128] / total[128:129]
    out[:128, :] = jnp.sqrt(measured[...]) / jnp.sqrt(model + intensity_offset) - 1.0
    out[128:, :] = total[136:]


def third_kernel(where, positions, f0, f1, f2, f3, patches, lit, probe, probes, psi0, psi, right, left, turn, rows128,
                 gkeep, gsend, keep, send, factor, canvas, q):
    table = (right, left, turn, rows128)
    y, zh, c = where[0], where[1], where[2]
    first = 4 * lax.rem(zh, 2) + 2 * c
    for s, f in enumerate((f0, f1, f2, f3)):
        factor[lax.rem(y + 4 - s, 4)] = f[:128, :]
    canvas[...] = jnp.zeros_like(canvas)
    waves = [(probe, psi0)] + [(probes.at[i], psi.at[i]) for i in range(3)]
    for f in range(2):
        fac = jnp.concatenate([factor[2 * f], factor[2 * f + 1]], axis=0)
        o_re, o_im = patches[f, 0], patches[f, 1]
        g_re = jnp.zeros((N, N), f32)
        g_im = jnp.zeros((N, N), f32)
        for i, (probe_ref, far) in enumerate(waves):
            re, im = restore(far[f, 0] * fac, far[f, 1] * fac, *table)
            p_re, p_im = probe_ref[0], probe_ref[1]
            g_re = g_re + (p_re * re + p_im * im)
            g_im = g_im + (p_re * im - p_im * re)
            q_re = o_re * re + o_im * im
            q_im = o_re * im - o_im * re
            if f == 0:
                q[0, i] = q_re
                q[1, i] = q_im
            else:
                q[0, i] += q_re
                q[1, i] += q_im
        base, down = split_row(positions[first + f, 0])
        col = positions[first + f, 1]
        for ch, g in enumerate((g_re, g_im)):
            tall = pltpu.roll(jnp.concatenate([g, jnp.zeros((TALL - N, N), f32)], axis=0), down, 0)
            wide = pltpu.roll(jnp.concatenate([tall, jnp.zeros((TALL, N), f32)], axis=1), col, 1)
            canvas[ch, pl.ds(base, TALL), :] += wide
    for ch in range(2):
        gkeep[ch] = canvas[ch, pl.ds(pl.multiple_of(c * N, N), N), :]
        gsend[ch] = canvas[ch, pl.ds(pl.multiple_of((1 - c) * N, N), N), :]
    for xc in range(4):
        for i in range(4):
            keep[xc, 64 * i:64 * i + 64, :] = q[c, i, 64 * xc:64 * xc + 64, :]
            send[xc, 64 * i:64 * i + 64, :] = q[1 - c, i, 64 * xc:64 * xc + 64, :]
        keep[xc, 256:, :] = lit[64 * xc:64 * xc + 64, :]
        send[xc, 256:, :] = lit[64 * xc:64 * xc + 64, :]


def fold_kernel(where, keep, got, o0, o1, o2, o3):
    for s, out in enumerate((o0, o1, o2, o3)):
        rows = pl.ds(pl.multiple_of(lax.rem(where[0] + s, 4) * 64, 64), 64)
        for ch in range(2):
            out[ch] = keep[ch, rows, :] + got[ch, rows, :]


def mix_kernel(where, keep, got, o0, o1, o2, o3):
    for s, out in enumerate((o0, o1, o2, o3)):
        j = lax.rem(where[3] + s, 4)
        out[...] = keep[j] + got[j]


def sum_kernel(where, g0, g1, g2, g3, own, out):
    odd = lax.rem(where[1], 2)
    for target, half in ((own, odd), (out, 1 - odd)):
        rows = pl.ds(pl.multiple_of(half * 32, 32), 32)
        for ch in range(2):
            target[ch] = (g0[ch, rows, :] + g1[ch, rows, :]) + (g2[ch, rows, :] + g3[ch, rows, :])


def rows_kernel(where, f0, f1, f2, f3, out):
    for s, f in enumerate((f0, f1, f2, f3)):
        out[pl.ds(pl.multiple_of(lax.rem(where[0] + 4 - s, 4) * 32, 32), 32), :] = f[128:, :]


def light_kernel(where, positions, near, far, out, padded):
    padded[:32, :] = jnp.zeros((32, N), f32)
    padded[pl.ds(pl.multiple_of(32 + 128 * where[2], 32), 128), :] = near[...]
    padded[pl.ds(pl.multiple_of(32 + 128 * (1 - where[2]), 32), 128), :] = far[...]
    padded[288:328, :] = jnp.zeros((40, N), f32)
    first = 256 * where[2] + 64 * where[0] + 32 * lax.rem(where[1], 2)
    total = jnp.zeros((32, SIDE), f32)
    for f in range(8):
        start = jnp.clip(first - positions[f, 0] + 32, 0, 288)
        base = start // 8 * 8
        rows = padded[pl.ds(pl.multiple_of(base, 8), 40), :]
        rows = pltpu.roll(rows, lax.rem(40 - (start - base), 40), 0)[:32]
        wide = jnp.concatenate([rows, jnp.zeros((32, N), f32)], axis=1)
        total = total + pltpu.roll(wide, positions[f, 1], 1)
    out[...] = total


def probe_sum_kernel(q0, q1, q2, q3, p0, p1, p2, p3, power):
    power[...] = (q0[256:, :] + q1[256:, :]) + (q2[256:, :] + q3[256:, :])
    for s, p in enumerate((p0, p1, p2, p3)):
        rows = slice(64 * s, 64 * s + 64)
        p[...] = (q0[rows, :] + q1[rows, :]) + (q2[rows, :] + q3[rows, :])


def update_kernel(own, got, obj, light, out):
    scale = light[...] + damping
    for ch in range(2):
        out[ch] = obj[ch] + (own[ch] + got[ch]) / scale


def probe_kernel(q0, q1, mine, new):
    new[...] = mine[...] + (q0[:64, :] + q1[:64, :]) / (q0[64:, :] + q1[64:, :] + damping)


def block_kernel(where, n0, n1, n2, n3, q0, q1, q2, q3, power, out, q):
    for s, n in enumerate((n0, n1, n2, n3)):
        source = lax.rem(where[1] + 4 - s, 4)
        rows = pl.ds(pl.multiple_of(lax.rem(source, 2) * 32, 32), 32)
        for ch in range(2):
            out[source // 2, ch, rows, :] = n[ch]
    q[:64, :] = (q0[...] + q1[...]) + (q2[...] + q3[...])
    q[64:, :] = power[...]


def split_kernel(where, b0, b1, b2, b3, n0, n1, n2, n3, keep, send, half):
    y, c, x = where[0], where[2], where[3]
    for s, (b, n) in enumerate(((b0, n0), (b1, n1), (b2, n2), (b3, n3))):
        rows = pl.ds(pl.multiple_of(lax.rem(y + 4 - s, 4) * 64, 64), 64)
        for ch in range(2):
            keep[ch, rows, :] = b[c, ch]
            send[ch, rows, :] = b[1 - c, ch]
        half[pl.ds(pl.multiple_of(lax.rem(x + 4 - s, 4) * 64, 64), 64), :] = n[...]


def last_kernel(where, keep, got, half, other, tile, probe):
    c = where[2]
    for ch in range(2):
        tile[ch, pl.ds(pl.multiple_of(c * N, N), N), :] = keep[ch]
        tile[ch, pl.ds(pl.multiple_of((1 - c) * N, N), N), :] = got[ch]
    probe[c] = half[...]
    probe[1 - c] = other[...]


def shift(x, axis, n, s):
    return lax.ppermute(x, axis, [(i, (i + s) % n) for i in range(n)])


def local(object_field, probes, measured, positions, weights):
    rights, lefts, turn, turn_rows = tables()
    forward, inverse = (
        tuple(jnp.asarray(t) for t in (rights[i], lefts[i], turn, turn_rows)) for i in range(2)
    )
    y, zh, c, x = (lax.axis_index(a) for a in ("y", "zh", "c", "x"))
    where = jnp.stack([y, zh, c, x]).astype(jnp.int32)
    probe = probes[0]
    steps = (1, 2, 3)

    def ring(parts, axis, sign=1):
        return [parts[0]] + [shift(parts[s], axis, 4, sign * s) for s in steps]

    def swap(value):
        return shift(value, "c", 2, 1)

    def small(kernel, name, ins, outs, *operands):
        return call(kernel, name, ins, outs, flops=10**6, nbytes=MiB)(*operands)

    own = lax.dynamic_index_in_dim(probe, c, 0, False)
    message = jnp.concatenate([own, jnp.broadcast_to(weights[:, None], (8, N))], axis=0)
    near = ring([message] * 4, "zh")

    mine = zh // 2 == c
    offsets = jnp.where(mine, positions[0, 0], swap(positions[0, 0]))
    other_tile = swap(object_field)
    place = 4 * (zh % 2) + y // 2
    frames = [lax.dynamic_index_in_dim(measured[0, 0], place + 2 * i, 0, False) for i in (c, 1 - c)]

    plane = (N, N)
    patches, power, lit, psi0, intensity = call(
        first_kernel, "first", [S, S, S, S] + [V] * 9,
        [(2, 2) + plane, (2,) + plane, plane, (2, 2) + plane, (H, N)],
        [pltpu.VMEM((SIDE, SIDE), f32)], flops=5 * 10**9, nbytes=6 * MiB,
    )(where, offsets, positions[0, 0], weights, object_field, other_tile, frames[0], swap(frames[1]), probe, *forward)

    near = [lax.optimization_barrier((m, power))[0] for m in near[1:]]
    far = [swap(m) for m in near]
    *sums, psi, others = call(
        second_kernel, "second", [S, S] + [V] * 13,
        [(168, N)] * 4 + [(3, 2, 2) + plane, (3, 2) + plane],
        [pltpu.VMEM((2,) + plane, f32), pltpu.VMEM((128, N), f32)], flops=15 * 10**9, nbytes=10 * MiB, limit=24,
    )(where, weights, patches, probe, power, *near, *far, *forward)

    (factor,) = small(factor_kernel, "factor", [V] * 5, [(160, N)], *ring(sums, "y"), intensity)
    factors = ring([factor] * 4, "y")

    gkeep, gsend, keep, send = call(
        third_kernel, "third", [S, S] + [V] * 14,
        [(2, N, SIDE)] * 2 + [(4, 320, N)] * 2,
        [pltpu.VMEM((4, 128, N), f32), pltpu.VMEM((2, SIDE, SIDE), f32), pltpu.VMEM((2, 4) + plane, f32)],
        flops=20 * 10**9, nbytes=14 * MiB, limit=36,
    )(where, offsets, *factors, patches, lit, probe, others, psi0, psi, *inverse)

    part = (2, 32, SIDE)
    folded = ring(small(fold_kernel, "fold", [S, V, V], [(2, 64, SIDE)] * 4, where, gkeep, swap(gsend)), "y")
    mixed = ring(small(mix_kernel, "mix", [S, V, V], [(320, N)] * 4, where, keep, swap(send)), "x")

    (rows,) = small(rows_kernel, "rows", [S] + [V] * 4, [(128, N)], where, *factors)
    (light,) = call(
        light_kernel, "light", [S, S, V, V], [(32, SIDE)], [pltpu.VMEM((328, N), f32)],
        flops=10**6, nbytes=MiB,
    )(where, offsets, rows, swap(rows))
    targets = [
        lax.dynamic_index_in_dim(t.reshape(2, 16, 32, SIDE), 8 * c + 2 * y + zh % 2, 1, False)
        for t in (object_field, other_tile)
    ]
    target = jnp.where(mine, *targets)
    own_rows = lax.dynamic_slice(probe, (c, 64 * x, 0), (1, 64, N))[0]

    own, out = small(sum_kernel, "sum", [S] + [V] * 4, [part] * 2, where, *folded)
    got = lax.ppermute(out, "zh", [(0, 1), (1, 0), (2, 3), (3, 2)])
    *qs, e = small(probe_sum_kernel, "probe_sum", [V] * 4, [(64, N)] * 5, *mixed)
    (new,) = small(update_kernel, "update", [V] * 4, [part], own, got, target, light)
    block, q = small(
        block_kernel, "block", [S] + [V] * 9, [(2, 2, 64, SIDE), (128, N)],
        where, *ring([new] * 4, "zh"), *ring(qs, "zh", -1), e,
    )
    blocks = ring([block] * 4, "y")
    (chunk,) = small(probe_kernel, "probe", [V] * 3, [(64, N)], q, shift(q, "zl", 2, 1), own_rows)
    chunks = ring([chunk] * 4, "x")
    keep, send, half = small(
        split_kernel, "split", [S] + [V] * 8, [(2, N, SIDE)] * 2 + [plane], where, *blocks, *chunks
    )
    new_object, new_probe = small(
        last_kernel, "last", [S] + [V] * 4, [(2, SIDE, SIDE), (2,) + plane],
        where, keep, swap(send), half, swap(half),
    )
    return new_object, new_probe[None]


def solution(mesh):
    inner = Mesh(mesh.devices.reshape(4, 4, 2, 2, 4), ("y", "zh", "zl", "c", "x"))
    wave, ty, tx = ("y", "zh"), ("zl", "c"), "x"
    in_specs = (
        P(None, ty, tx),
        P(wave, None, None, None),
        P(ty, tx, None, None, None),
        P(ty, tx, None, None),
        P(wave),
    )
    out_specs = (P(None, ty, tx), P(wave, None, None, None))
    return jax.shard_map(local, mesh=inner, in_specs=in_specs, out_specs=out_specs, check_vma=False)
```

```python
import math

import jax
import jax.numpy as jnp
import ml_dtypes
import numpy as np
from jax import lax
from jax.experimental import pallas as pl
from jax.experimental.pallas import tpu as pltpu
from jax.sharding import Mesh
from jax.sharding import PartitionSpec as P

f32 = jnp.float32
bf16 = jnp.bfloat16
damping = 1.0
intensity_offset = 0.1
N = 256
H = 128
SIDE = 512
TALL = 264


def tables():
    k = np.arange(H)
    angle = 2.0 * math.pi / H * (np.outer(k, k) % H)
    c, s = np.cos(angle) / 16.0, -np.sin(angle) / 16.0
    forward, inverse = np.block([[c, -s], [s, c]]), np.block([[c, s], [-s, c]])

    def split(table, axis):
        high = table.astype(np.float32).astype(ml_dtypes.bfloat16)
        low = (table - high.astype(np.float64)).astype(np.float32).astype(ml_dtypes.bfloat16)
        return np.concatenate([high, high, low], axis=axis)

    turn = np.exp(-2j * math.pi * k / N)
    turn = np.stack([turn.real, turn.imag]).astype(np.float32)
    rows = np.broadcast_to(turn[:, :, None], (2, H, H)).copy()
    return [split(t.T, 0) for t in (forward, inverse)], [split(t, 1) for t in (forward, inverse)], turn, rows


def split_data(x, axis):
    high = x.astype(bf16)
    low = (x - high.astype(f32)).astype(bf16)
    return jnp.concatenate([high, low, high], axis=axis)


def cat(parts, axis):
    return jnp.concatenate(parts, axis=axis)


def twiddle(re, im, wr, wi):
    return re * wr - im * wi, re * wi + im * wr


def transform(re, im, right, left, turn, rows):
    a, b, ai, bi = re[:, :H], re[:, H:], im[:, :H], im[:, H:]
    o_re, o_im = twiddle(a - b, ai - bi, turn[0:1, :], turn[1:2, :])
    x = cat([cat([a + b, ai + bi], 1), cat([o_re, o_im], 1)], 0)
    x = jnp.dot(split_data(x, 1), right[...], preferred_element_type=f32)
    re, im = cat([x[:N, :H], x[N:, :H]], 1), cat([x[:N, H:], x[N:, H:]], 1)
    a, b, ai, bi = re[:H], re[H:], im[:H], im[H:]
    wr, wi = cat([rows[0]] * 2, 1), cat([rows[1]] * 2, 1)
    o_re, o_im = twiddle(a - b, ai - bi, wr, wi)
    x = cat([cat([a + b, ai + bi], 0), cat([o_re, o_im], 0)], 1)
    x = jnp.dot(left[...], split_data(x, 0), preferred_element_type=f32)
    return cat([x[:H, :N], x[:H, N:]], 0), cat([x[H:, :N], x[H:, N:]], 0)


def restore(re, im, right, left, turn, rows):
    x = cat([cat([re[:, :H], im[:, :H]], 1), cat([re[:, H:], im[:, H:]], 1)], 0)
    x = jnp.dot(split_data(x, 1), right[...], preferred_element_type=f32)
    o_re, o_im = twiddle(x[N:, :H], x[N:, H:], turn[0:1, :], -turn[1:2, :])
    e_re, e_im = x[:N, :H], x[:N, H:]
    re, im = cat([e_re + o_re, e_re - o_re], 1), cat([e_im + o_im, e_im - o_im], 1)
    x = cat([cat([re[:H], im[:H]], 0), cat([re[H:], im[H:]], 0)], 1)
    x = jnp.dot(left[...], split_data(x, 0), preferred_element_type=f32)
    wr, wi = cat([rows[0]] * 2, 1), -cat([rows[1]] * 2, 1)
    o_re, o_im = twiddle(x[:H, N:], x[H:, N:], wr, wi)
    e_re, e_im = x[:H, :N], x[H:, :N]
    return cat([e_re + o_re, e_re - o_re], 0), cat([e_im + o_im, e_im - o_im], 0)


def split_row(row):
    base = pl.multiple_of(jnp.minimum(row // 8 * 8, SIDE - TALL), 8)
    return base, row - base


def spec(space=pltpu.VMEM):
    return pl.BlockSpec(memory_space=space)


def call(kernel, name, ins, outs, scratch=(), flops=0, nbytes=0, limit=16):
    return pl.pallas_call(
        kernel,
        name=name,
        out_shape=[jax.ShapeDtypeStruct(o, f32) for o in outs],
        in_specs=ins,
        out_specs=[spec() for _ in outs],
        scratch_shapes=list(scratch),
        compiler_params=pltpu.CompilerParams(vmem_limit_bytes=limit * MiB),
        cost_estimate=pl.CostEstimate(flops=flops, bytes_accessed=nbytes, transcendentals=0),
    )


V = spec()
S = spec(pltpu.SMEM)
A = spec(pl.ANY)
MiB = 1 << 20


def pick(frame, parity):
    i, r = lax.broadcasted_iota(jnp.int32, (H, N), 0), lax.broadcasted_iota(jnp.int32, (H, N), 1)
    pick_rows = jnp.where(r == 2 * i + parity, 1.0, 0.0).astype(bf16)
    r, j = lax.broadcasted_iota(jnp.int32, (N, N), 0), lax.broadcasted_iota(jnp.int32, (N, N), 1)
    pick_columns = jnp.where(r == jnp.where(j < H, 2 * j, 2 * j - (N - 1)), 1.0, 0.0).astype(bf16)
    rest = frame
    total = jnp.zeros((H, N), f32)
    for _ in range(3):
        part = rest.astype(bf16)
        rest = rest - part.astype(f32)
        part = jnp.dot(pick_rows, part, preferred_element_type=f32).astype(bf16)
        total = total + jnp.dot(part, pick_columns, preferred_element_type=f32)
    return total


def first_kernel(where, positions, own_positions, weight, obj, got, measured, got_measured, probe, right, left, turn, rows128,
                 patches, power, total, psi, intensity, squares, frames, sems):
    table = (right, left, turn, rows128)
    y, zh, c = where[0], where[1], where[2]
    mine = zh // 2 == c
    w = weight[0]
    first = 4 * lax.rem(zh, 2) + 2 * c

    copies = []
    for i, source in enumerate((measured, got_measured)):
        copies.append(pltpu.make_async_copy(source.at[first + y // 2], frames.at[i], sems.at[i]))
        copies[i].start()

    def window(source, row, col):
        base, down = split_row(row)
        part = pltpu.roll(source[pl.ds(base, TALL), :], lax.rem(SIDE - col, SIDE), 1)[:, :N]
        return pltpu.roll(part, lax.rem(TALL - down, TALL), 0)[:N]

    def take(source):
        for f in range(2):
            for ch in range(2):
                patches[f, ch] = window(source.at[ch], positions[first + f, 0], positions[first + f, 1])

    @pl.when(mine)
    def _():
        take(obj)

    @pl.when(jnp.logical_not(mine))
    def _():
        take(got)

    for f in range(2):
        o_re, o_im = patches[f, 0], patches[f, 1]
        p_re, p_im = probe[0], probe[1]
        re, im = transform(p_re * o_re - p_im * o_im, p_re * o_im + p_im * o_re, *table)
        psi[f, 0] = re
        psi[f, 1] = im
        power[f] = w * (re * re + im * im)
    squares[...] = obj[0] * obj[0] + obj[1] * obj[1]
    lit = jnp.zeros((N, N), f32)
    for f in range(8):
        lit = lit + window(squares, own_positions[f, 0], own_positions[f, 1])
    total[...] = lit
    flag = jnp.full((1, N), zh // 2 - c, jnp.int32) == 0
    for copy in copies:
        copy.wait()
    intensity[...] = pick(jnp.where(flag, frames[0], frames[1]), lax.rem(y, 2))


def more_waves(where, patches, arrivals, table, power, psi, probes):
    c = where[2]
    flag = jnp.full((1, N), c, jnp.int32) == 0
    mine = pl.ds(pl.multiple_of(128 * c, 128), 128)
    wsum = jnp.zeros((8, N), f32)
    light = jnp.zeros((128, N), f32)
    for i, (a, b) in enumerate(arrivals):
        own, other = a[:N, :], b[:N, :]
        p_re, p_im = jnp.where(flag, own, other), jnp.where(flag, other, own)
        probes[i, 0] = p_re
        probes[i, 1] = p_im
        wsum = wsum + a[N:, :]
        w = a[N:N + 1, :]
        for f in range(2):
            o_re, o_im = patches[f, 0], patches[f, 1]
            re, im = transform(p_re * o_re - p_im * o_im, p_re * o_im + p_im * o_re, *table)
            psi[i, f, 0] = re
            psi[i, f, 1] = im
            power[f] += w * (re * re + im * im)
        re, im = probes[i, 0, mine, :], probes[i, 1, mine, :]
        light = light + (re * re + im * im)
    return wsum, light


def second_kernel(where, weight, patches, probe, power0, a1, a2, a3, b1, b2, b3, right, left, turn, rows128,
                  out0, out1, out2, out3, psi, probes, power, lights):
    power[...] = power0[...]
    wsum, light = more_waves(
        where, patches, ((a1, b1), (a2, b2), (a3, b3)), (right, left, turn, rows128), power, psi, probes
    )
    wsum = wsum + weight[0]
    mine = pl.ds(pl.multiple_of(128 * where[2], 128), 128)
    re, im = probe[0, mine, :], probe[1, mine, :]
    lights[...] = light + (re * re + im * im)
    for s, out in enumerate((out0, out1, out2, out3)):
        j = lax.rem(where[0] + s, 4)
        out[:128, :] = power[j // 2, pl.ds(pl.multiple_of((j % 2) * 128, 128), 128), :]
        out[128:136, :] = wsum
        out[136:168, :] = lights[pl.ds(pl.multiple_of(32 * j, 32), 32), :]


def factor_kernel(m0, m1, m2, m3, measured, out):
    total = (m0[...] + m1[...]) + (m2[...] + m3[...])
    model = total[:128] / total[128:129]
    out[:128, :] = jnp.sqrt(measured[...]) / jnp.sqrt(model + intensity_offset) - 1.0
    out[128:, :] = total[136:]


def third_kernel(where, positions, f0, f1, f2, f3, patches, lit, probe, probes, psi0, psi, right, left, turn, rows128,
                 gkeep, gsend, keep, send, factor, canvas, q):
    table = (right, left, turn, rows128)
    y, zh, c = where[0], where[1], where[2]
    first = 4 * lax.rem(zh, 2) + 2 * c
    for s, f in enumerate((f0, f1, f2, f3)):
        factor[lax.rem(y + 4 - s, 4)] = f[:128, :]
    canvas[...] = jnp.zeros_like(canvas)
    waves = [(probe, psi0)] + [(probes.at[i], psi.at[i]) for i in range(3)]
    for f in range(2):
        fac = jnp.concatenate([factor[2 * f], factor[2 * f + 1]], axis=0)
        o_re, o_im = patches[f, 0], patches[f, 1]
        g_re = jnp.zeros((N, N), f32)
        g_im = jnp.zeros((N, N), f32)
        for i, (probe_ref, far) in enumerate(waves):
            re, im = restore(far[f, 0] * fac, far[f, 1] * fac, *table)
            p_re, p_im = probe_ref[0], probe_ref[1]
            g_re = g_re + (p_re * re + p_im * im)
            g_im = g_im + (p_re * im - p_im * re)
            q_re = o_re * re + o_im * im
            q_im = o_re * im - o_im * re
            if f == 0:
                q[0, i] = q_re
                q[1, i] = q_im
            else:
                q[0, i] += q_re
                q[1, i] += q_im
        base, down = split_row(positions[first + f, 0])
        col = positions[first + f, 1]
        for ch, g in enumerate((g_re, g_im)):
            tall = pltpu.roll(jnp.concatenate([g, jnp.zeros((TALL - N, N), f32)], axis=0), down, 0)
            wide = pltpu.roll(jnp.concatenate([tall, jnp.zeros((TALL, N), f32)], axis=1), col, 1)
            canvas[ch, pl.ds(base, TALL), :] += wide
    for ch in range(2):
        gkeep[ch] = canvas[ch, pl.ds(pl.multiple_of(c * N, N), N), :]
        gsend[ch] = canvas[ch, pl.ds(pl.multiple_of((1 - c) * N, N), N), :]
    for xc in range(4):
        for i in range(4):
            keep[xc, 64 * i:64 * i + 64, :] = q[c, i, 64 * xc:64 * xc + 64, :]
            send[xc, 64 * i:64 * i + 64, :] = q[1 - c, i, 64 * xc:64 * xc + 64, :]
        keep[xc, 256:, :] = lit[64 * xc:64 * xc + 64, :]
        send[xc, 256:, :] = lit[64 * xc:64 * xc + 64, :]


def fold_kernel(where, keep, got, o0, o1, o2, o3):
    for s, out in enumerate((o0, o1, o2, o3)):
        rows = pl.ds(pl.multiple_of(lax.rem(where[0] + s, 4) * 64, 64), 64)
        for ch in range(2):
            out[ch] = keep[ch, rows, :] + got[ch, rows, :]


def mix_kernel(where, keep, got, o0, o1, o2, o3):
    for s, out in enumerate((o0, o1, o2, o3)):
        j = lax.rem(where[3] + s, 4)
        out[...] = keep[j] + got[j]


def sum_kernel(where, g0, g1, g2, g3, own, out):
    odd = lax.rem(where[1], 2)
    for target, half in ((own, odd), (out, 1 - odd)):
        rows = pl.ds(pl.multiple_of(half * 32, 32), 32)
        for ch in range(2):
            target[ch] = (g0[ch, rows, :] + g1[ch, rows, :]) + (g2[ch, rows, :] + g3[ch, rows, :])


def rows_kernel(where, f0, f1, f2, f3, out):
    for s, f in enumerate((f0, f1, f2, f3)):
        out[pl.ds(pl.multiple_of(lax.rem(where[0] + 4 - s, 4) * 32, 32), 32), :] = f[128:, :]


def light_kernel(where, positions, near, far, out, padded):
    padded[:32, :] = jnp.zeros((32, N), f32)
    padded[pl.ds(pl.multiple_of(32 + 128 * where[2], 32), 128), :] = near[...]
    padded[pl.ds(pl.multiple_of(32 + 128 * (1 - where[2]), 32), 128), :] = far[...]
    padded[288:328, :] = jnp.zeros((40, N), f32)
    first = 256 * where[2] + 64 * where[0] + 32 * lax.rem(where[1], 2)
    total = jnp.zeros((32, SIDE), f32)
    for f in range(8):
        start = jnp.clip(first - positions[f, 0] + 32, 0, 288)
        base = start // 8 * 8
        rows = padded[pl.ds(pl.multiple_of(base, 8), 40), :]
        rows = pltpu.roll(rows, lax.rem(40 - (start - base), 40), 0)[:32]
        wide = jnp.concatenate([rows, jnp.zeros((32, N), f32)], axis=1)
        total = total + pltpu.roll(wide, positions[f, 1], 1)
    out[...] = total


def probe_sum_kernel(q0, q1, q2, q3, p0, p1, p2, p3, power):
    power[...] = (q0[256:, :] + q1[256:, :]) + (q2[256:, :] + q3[256:, :])
    for s, p in enumerate((p0, p1, p2, p3)):
        rows = slice(64 * s, 64 * s + 64)
        p[...] = (q0[rows, :] + q1[rows, :]) + (q2[rows, :] + q3[rows, :])


def update_kernel(own, got, obj, light, out):
    scale = light[...] + damping
    for ch in range(2):
        out[ch] = obj[ch] + (own[ch] + got[ch]) / scale


def block_kernel(where, n0, n1, n2, n3, f0, f1, f2, f3, out):
    c = where[2]
    for s, (n, f) in enumerate(((n0, f0), (n1, f1), (n2, f2), (n3, f3))):
        source = lax.rem(where[1] + 4 - s, 4)
        rows = pl.ds(pl.multiple_of(lax.rem(source, 2) * 32, 32), 32)

        @pl.when(source // 2 == c)
        def _():
            for ch in range(2):
                out[c, ch, rows, :] = n[ch]
                out[1 - c, ch, rows, :] = f[ch]


def pack_kernel(q0, q1, q2, q3, power, q):
    q[:64, :] = (q0[...] + q1[...]) + (q2[...] + q3[...])
    q[64:, :] = power[...]


def probe_kernel(q0, q1, mine, new):
    new[...] = mine[...] + (q0[:64, :] + q1[:64, :]) / (q0[64:, :] + q1[64:, :] + damping)


def half_kernel(where, n0, n1, n2, n3, half):
    for s, n in enumerate((n0, n1, n2, n3)):
        half[pl.ds(pl.multiple_of(lax.rem(where[3] + 4 - s, 4) * 64, 64), 64), :] = n[...]


def last_kernel(where, b0, b1, b2, b3, half, other, tile, probe):
    y, c = where[0], where[2]
    for s, b in enumerate((b0, b1, b2, b3)):
        start = lax.rem(y + 4 - s, 4) * 64
        for i in range(2):
            for ch in range(2):
                tile[ch, pl.ds(pl.multiple_of(start + i * N, 64), 64), :] = b[i, ch]
    probe[c] = half[...]
    probe[1 - c] = other[...]


def shift(x, axis, n, s):
    return lax.ppermute(x, axis, [(i, (i + s) % n) for i in range(n)])


def local(object_field, probes, measured, positions, weights):
    rights, lefts, turn, turn_rows = tables()
    forward, inverse = (
        tuple(jnp.asarray(t) for t in (rights[i], lefts[i], turn, turn_rows)) for i in range(2)
    )
    y, zh, c, x = (lax.axis_index(a) for a in ("y", "zh", "c", "x"))
    where = jnp.stack([y, zh, c, x]).astype(jnp.int32)
    probe = probes[0]
    steps = (1, 2, 3)

    def ring(parts, axis, sign=1):
        return [parts[0]] + [shift(parts[s], axis, 4, sign * s) for s in steps]

    def swap(value):
        return shift(value, "c", 2, 1)

    def small(kernel, name, ins, outs, *operands):
        return call(kernel, name, ins, outs, flops=10**6, nbytes=MiB)(*operands)

    padded = [lax.pad(probe[ch], weights[0], ((0, 8, 0), (0, 0, 0))) for ch in range(2)]
    message = jnp.where(c == 0, *padded)
    near = ring([message] * 4, "zh")

    mine = zh // 2 == c
    offsets = jnp.where(mine, positions[0, 0], swap(positions[0, 0]))
    other_tile = swap(object_field)

    plane = (N, N)
    patches, power, lit, psi0, intensity = call(
        first_kernel, "first", [S, S, S, S, V, V, A, A] + [V] * 5,
        [(2, 2) + plane, (2,) + plane, plane, (2, 2) + plane, (H, N)],
        [pltpu.VMEM((SIDE, SIDE), f32), pltpu.VMEM((2, N, N), f32), pltpu.SemaphoreType.DMA((2,))],
        flops=5 * 10**9, nbytes=6 * MiB,
    )(where, offsets, positions[0, 0], weights, object_field, other_tile, measured[0, 0], swap(measured[0, 0]), probe, *forward)

    near = [lax.optimization_barrier((m, power))[0] for m in near[1:]]
    far = [swap(m) for m in near]
    *sums, psi, others = call(
        second_kernel, "second", [S, S] + [V] * 13,
        [(168, N)] * 4 + [(3, 2, 2) + plane, (3, 2) + plane],
        [pltpu.VMEM((2,) + plane, f32), pltpu.VMEM((128, N), f32)], flops=15 * 10**9, nbytes=10 * MiB, limit=24,
    )(where, weights, patches, probe, power, *near, *far, *forward)

    (factor,) = small(factor_kernel, "factor", [V] * 5, [(160, N)], *ring(sums, "y"), intensity)
    factors = ring([factor] * 4, "y")

    gkeep, gsend, keep, send = call(
        third_kernel, "third", [S, S] + [V] * 14,
        [(2, N, SIDE)] * 2 + [(4, 320, N)] * 2,
        [pltpu.VMEM((4, 128, N), f32), pltpu.VMEM((2, SIDE, SIDE), f32), pltpu.VMEM((2, 4) + plane, f32)],
        flops=20 * 10**9, nbytes=14 * MiB, limit=36,
    )(where, offsets, *factors, patches, lit, probe, others, psi0, psi, *inverse)

    part = (2, 32, SIDE)
    gswapped = swap(gsend)
    send = lax.optimization_barrier((send, gswapped))[0]
    folded = ring(small(fold_kernel, "fold", [S, V, V], [(2, 64, SIDE)] * 4, where, gkeep, gswapped), "y")
    mixed = ring(small(mix_kernel, "mix", [S, V, V], [(320, N)] * 4, where, keep, swap(send)), "x")

    (rows,) = small(rows_kernel, "rows", [S] + [V] * 4, [(128, N)], where, *factors)
    (light,) = call(
        light_kernel, "light", [S, S, V, V], [(32, SIDE)], [pltpu.VMEM((328, N), f32)],
        flops=10**6, nbytes=MiB,
    )(where, offsets, rows, swap(rows))
    targets = [
        lax.dynamic_index_in_dim(t.reshape(2, 16, 32, SIDE), 8 * c + 2 * y + zh % 2, 1, False)
        for t in (object_field, other_tile)
    ]
    target = jnp.where(mine, *targets)
    own_rows = lax.dynamic_slice(probe, (c, 64 * x, 0), (1, 64, N))[0]

    own, out = small(sum_kernel, "sum", [S] + [V] * 4, [part] * 2, where, *folded)
    got = lax.ppermute(out, "zh", [(0, 1), (1, 0), (2, 3), (3, 2)])
    *qs, e = small(probe_sum_kernel, "probe_sum", [V] * 4, [(64, N)] * 5, *mixed)
    got = lax.optimization_barrier((got, e))[0]
    (new,) = small(update_kernel, "update", [V] * 4, [part], own, got, target, light)
    new = ring([new] * 4, "zh")
    (q,) = small(pack_kernel, "pack", [V] * 5, [(128, N)], *ring(qs, "zh", -1), e)
    crossed = [swap(new[0])] + [swap(lax.optimization_barrier((n, q))[0]) for n in new[1:]]
    (block,) = small(block_kernel, "block", [S] + [V] * 8, [(2, 2, 64, SIDE)], where, *new, *crossed)
    blocks = ring([block] * 4, "y")
    (chunk,) = small(probe_kernel, "probe", [V] * 3, [(64, N)], q, shift(q, "zl", 2, 1), own_rows)
    (half,) = small(half_kernel, "half", [S] + [V] * 4, [plane], where, *ring([chunk] * 4, "x"))
    new_object, new_probe = small(
        last_kernel, "last", [S] + [V] * 6, [(2, SIDE, SIDE), (2,) + plane], where, *blocks, half, swap(half)
    )
    return new_object, new_probe[None]


def solution(mesh):
    inner = Mesh(mesh.devices.reshape(4, 4, 2, 2, 4), ("y", "zh", "zl", "c", "x"))
    wave, ty, tx = ("y", "zh"), ("zl", "c"), "x"
    in_specs = (
        P(None, ty, tx),
        P(wave, None, None, None),
        P(ty, tx, None, None, None),
        P(ty, tx, None, None),
        P(wave),
    )
    out_specs = (P(None, ty, tx), P(wave, None, None, None))
    return jax.shard_map(local, mesh=inner, in_specs=in_specs, out_specs=out_specs, check_vma=False)
```

```python
import math

import jax
import jax.numpy as jnp
import ml_dtypes
import numpy as np
from jax import lax
from jax.experimental import pallas as pl
from jax.experimental.pallas import tpu as pltpu
from jax.sharding import Mesh
from jax.sharding import PartitionSpec as P

f32 = jnp.float32
bf16 = jnp.bfloat16
damping = 1.0
intensity_offset = 0.1
N = 256
H = 128
SIDE = 512
TALL = 264


def tables():
    k = np.arange(H)
    angle = 2.0 * math.pi / H * (np.outer(k, k) % H)
    c, s = np.cos(angle) / 16.0, -np.sin(angle) / 16.0
    forward, inverse = np.block([[c, -s], [s, c]]), np.block([[c, s], [-s, c]])

    def split(table, axis):
        high = table.astype(np.float32).astype(ml_dtypes.bfloat16)
        low = (table - high.astype(np.float64)).astype(np.float32).astype(ml_dtypes.bfloat16)
        return np.concatenate([high, high, low], axis=axis)

    turn = np.exp(-2j * math.pi * k / N)
    turn = np.stack([turn.real, turn.imag]).astype(np.float32)
    rows = np.broadcast_to(turn[:, :, None], (2, H, H)).copy()
    return [split(t.T, 0) for t in (forward, inverse)], [split(t, 1) for t in (forward, inverse)], turn, rows


def split_data(x, axis):
    high = x.astype(bf16)
    low = (x - high.astype(f32)).astype(bf16)
    return jnp.concatenate([high, low, high], axis=axis)


def cat(parts, axis):
    return jnp.concatenate(parts, axis=axis)


def twiddle(re, im, wr, wi):
    return re * wr - im * wi, re * wi + im * wr


def transform(re, im, right, left, turn, rows):
    a, b, ai, bi = re[:, :H], re[:, H:], im[:, :H], im[:, H:]
    o_re, o_im = twiddle(a - b, ai - bi, turn[0:1, :], turn[1:2, :])
    x = cat([cat([a + b, ai + bi], 1), cat([o_re, o_im], 1)], 0)
    x = jnp.dot(split_data(x, 1), right[...], preferred_element_type=f32)
    re, im = cat([x[:N, :H], x[N:, :H]], 1), cat([x[:N, H:], x[N:, H:]], 1)
    a, b, ai, bi = re[:H], re[H:], im[:H], im[H:]
    wr, wi = cat([rows[0]] * 2, 1), cat([rows[1]] * 2, 1)
    o_re, o_im = twiddle(a - b, ai - bi, wr, wi)
    x = cat([cat([a + b, ai + bi], 0), cat([o_re, o_im], 0)], 1)
    x = jnp.dot(left[...], split_data(x, 0), preferred_element_type=f32)
    return cat([x[:H, :N], x[:H, N:]], 0), cat([x[H:, :N], x[H:, N:]], 0)


def restore(re, im, right, left, turn, rows):
    x = cat([cat([re[:, :H], im[:, :H]], 1), cat([re[:, H:], im[:, H:]], 1)], 0)
    x = jnp.dot(split_data(x, 1), right[...], preferred_element_type=f32)
    o_re, o_im = twiddle(x[N:, :H], x[N:, H:], turn[0:1, :], -turn[1:2, :])
    e_re, e_im = x[:N, :H], x[:N, H:]
    re, im = cat([e_re + o_re, e_re - o_re], 1), cat([e_im + o_im, e_im - o_im], 1)
    x = cat([cat([re[:H], im[:H]], 0), cat([re[H:], im[H:]], 0)], 1)
    x = jnp.dot(left[...], split_data(x, 0), preferred_element_type=f32)
    wr, wi = cat([rows[0]] * 2, 1), -cat([rows[1]] * 2, 1)
    o_re, o_im = twiddle(x[:H, N:], x[H:, N:], wr, wi)
    e_re, e_im = x[:H, :N], x[H:, :N]
    return cat([e_re + o_re, e_re - o_re], 0), cat([e_im + o_im, e_im - o_im], 0)


def split_row(row):
    base = pl.multiple_of(jnp.minimum(row // 8 * 8, SIDE - TALL), 8)
    return base, row - base


def spec(space=pltpu.VMEM):
    return pl.BlockSpec(memory_space=space)


def call(kernel, name, ins, outs, scratch=(), flops=0, nbytes=0, limit=16):
    return pl.pallas_call(
        kernel,
        name=name,
        out_shape=[jax.ShapeDtypeStruct(o, f32) for o in outs],
        in_specs=ins,
        out_specs=[spec() for _ in outs],
        scratch_shapes=list(scratch),
        compiler_params=pltpu.CompilerParams(vmem_limit_bytes=limit * MiB),
        cost_estimate=pl.CostEstimate(flops=flops, bytes_accessed=nbytes, transcendentals=0),
    )


V = spec()
S = spec(pltpu.SMEM)
MiB = 1 << 20


def pick(frame, parity):
    i, r = lax.broadcasted_iota(jnp.int32, (H, N), 0), lax.broadcasted_iota(jnp.int32, (H, N), 1)
    pick_rows = jnp.where(r == 2 * i + parity, 1.0, 0.0).astype(bf16)
    r, j = lax.broadcasted_iota(jnp.int32, (N, N), 0), lax.broadcasted_iota(jnp.int32, (N, N), 1)
    pick_columns = jnp.where(r == jnp.where(j < H, 2 * j, 2 * j - (N - 1)), 1.0, 0.0).astype(bf16)
    rest = frame
    total = jnp.zeros((H, N), f32)
    for _ in range(3):
        part = rest.astype(bf16)
        rest = rest - part.astype(f32)
        part = jnp.dot(pick_rows, part, preferred_element_type=f32).astype(bf16)
        total = total + jnp.dot(part, pick_columns, preferred_element_type=f32)
    return total


def first_kernel(where, positions, own_positions, weight, obj, got, frame, got_frame, probe, right, left, turn, rows128,
                 patches, power, total, psi, intensity, squares):
    table = (right, left, turn, rows128)
    y, zh, c = where[0], where[1], where[2]
    mine = zh // 2 == c
    w = weight[0]
    first = 4 * lax.rem(zh, 2) + 2 * c

    def window(source, row, col):
        base, down = split_row(row)
        part = pltpu.roll(source[pl.ds(base, TALL), :], lax.rem(SIDE - col, SIDE), 1)[:, :N]
        return pltpu.roll(part, lax.rem(TALL - down, TALL), 0)[:N]

    def take(source):
        for f in range(2):
            for ch in range(2):
                patches[f, ch] = window(source.at[ch], positions[first + f, 0], positions[first + f, 1])

    @pl.when(mine)
    def _():
        take(obj)

    @pl.when(jnp.logical_not(mine))
    def _():
        take(got)

    for f in range(2):
        o_re, o_im = patches[f, 0], patches[f, 1]
        p_re, p_im = probe[0], probe[1]
        re, im = transform(p_re * o_re - p_im * o_im, p_re * o_im + p_im * o_re, *table)
        psi[f, 0] = re
        psi[f, 1] = im
        power[f] = w * (re * re + im * im)
    squares[...] = obj[0] * obj[0] + obj[1] * obj[1]
    lit = jnp.zeros((N, N), f32)
    for f in range(8):
        lit = lit + window(squares, own_positions[f, 0], own_positions[f, 1])
    total[...] = lit
    flag = jnp.full((1, N), zh // 2 - c, jnp.int32) == 0
    intensity[...] = pick(jnp.where(flag, frame[...], got_frame[...]), lax.rem(y, 2))


def more_waves(where, patches, arrivals, table, power, psi, probes):
    c = where[2]
    flag = jnp.full((1, N), c, jnp.int32) == 0
    mine = pl.ds(pl.multiple_of(128 * c, 128), 128)
    wsum = jnp.zeros((8, N), f32)
    light = jnp.zeros((128, N), f32)
    for i, (a, b) in enumerate(arrivals):
        own, other = a[:N, :], b[:N, :]
        p_re, p_im = jnp.where(flag, own, other), jnp.where(flag, other, own)
        probes[i, 0] = p_re
        probes[i, 1] = p_im
        wsum = wsum + a[N:, :]
        w = a[N:N + 1, :]
        for f in range(2):
            o_re, o_im = patches[f, 0], patches[f, 1]
            re, im = transform(p_re * o_re - p_im * o_im, p_re * o_im + p_im * o_re, *table)
            psi[i, f, 0] = re
            psi[i, f, 1] = im
            power[f] += w * (re * re + im * im)
        re, im = probes[i, 0, mine, :], probes[i, 1, mine, :]
        light = light + (re * re + im * im)
    return wsum, light


def second_kernel(where, weight, patches, probe, power0, a1, a2, a3, b1, b2, b3, right, left, turn, rows128,
                  out0, out1, out2, out3, psi, probes, power, lights):
    power[...] = power0[...]
    wsum, light = more_waves(
        where, patches, ((a1, b1), (a2, b2), (a3, b3)), (right, left, turn, rows128), power, psi, probes
    )
    wsum = wsum + weight[0]
    mine = pl.ds(pl.multiple_of(128 * where[2], 128), 128)
    re, im = probe[0, mine, :], probe[1, mine, :]
    lights[...] = light + (re * re + im * im)
    for s, out in enumerate((out0, out1, out2, out3)):
        j = lax.rem(where[0] + s, 4)
        out[:128, :] = power[j // 2, pl.ds(pl.multiple_of((j % 2) * 128, 128), 128), :]
        out[128:136, :] = wsum
        out[136:168, :] = lights[pl.ds(pl.multiple_of(32 * j, 32), 32), :]


def factor_kernel(m0, m1, m2, m3, measured, out):
    total = (m0[...] + m1[...]) + (m2[...] + m3[...])
    model = total[:128] / total[128:129]
    out[:128, :] = jnp.sqrt(measured[...]) / jnp.sqrt(model + intensity_offset) - 1.0
    out[128:, :] = total[136:]


def third_kernel(where, positions, f0, f1, f2, f3, probe, probes, psi0, psi, right, left, turn, rows128,
                 gkeep, gsend, chi, factor, canvas):
    table = (right, left, turn, rows128)
    y, zh, c = where[0], where[1], where[2]
    first = 4 * lax.rem(zh, 2) + 2 * c
    for s, f in enumerate((f0, f1, f2, f3)):
        factor[lax.rem(y + 4 - s, 4)] = f[:128, :]
    canvas[...] = jnp.zeros_like(canvas)
    waves = [(probe, psi0)] + [(probes.at[i], psi.at[i]) for i in range(3)]
    for f in range(2):
        fac = jnp.concatenate([factor[2 * f], factor[2 * f + 1]], axis=0)
        g_re = jnp.zeros((N, N), f32)
        g_im = jnp.zeros((N, N), f32)
        for i, (probe_ref, far) in enumerate(waves):
            re, im = restore(far[f, 0] * fac, far[f, 1] * fac, *table)
            p_re, p_im = probe_ref[0], probe_ref[1]
            g_re = g_re + (p_re * re + p_im * im)
            g_im = g_im + (p_re * im - p_im * re)
            chi[f, i, 0] = re
            chi[f, i, 1] = im
        base, down = split_row(positions[first + f, 0])
        col = positions[first + f, 1]
        for ch, g in enumerate((g_re, g_im)):
            tall = pltpu.roll(jnp.concatenate([g, jnp.zeros((TALL - N, N), f32)], axis=0), down, 0)
            wide = pltpu.roll(jnp.concatenate([tall, jnp.zeros((TALL, N), f32)], axis=1), col, 1)
            canvas[ch, pl.ds(base, TALL), :] += wide
    for ch in range(2):
        gkeep[ch] = canvas[ch, pl.ds(pl.multiple_of(c * N, N), N), :]
        gsend[ch] = canvas[ch, pl.ds(pl.multiple_of((1 - c) * N, N), N), :]


def fourth_kernel(where, patches, chi, lit, keep, send, q):
    c = where[2]
    for i in range(4):
        re, im = jnp.zeros((N, N), f32), jnp.zeros((N, N), f32)
        for f in range(2):
            o_re, o_im, a, b = patches[f, 0], patches[f, 1], chi[f, i, 0], chi[f, i, 1]
            re = re + (o_re * a + o_im * b)
            im = im + (o_re * b - o_im * a)
        q[0] = re
        q[1] = im
        for xc in range(4):
            keep[xc, 64 * i:64 * i + 64, :] = q[c, 64 * xc:64 * xc + 64, :]
            send[xc, 64 * i:64 * i + 64, :] = q[1 - c, 64 * xc:64 * xc + 64, :]
    for xc in range(4):
        keep[xc, 256:, :] = lit[64 * xc:64 * xc + 64, :]
        send[xc, 256:, :] = lit[64 * xc:64 * xc + 64, :]


def fold_kernel(where, keep, got, o0, o1, o2, o3):
    for s, out in enumerate((o0, o1, o2, o3)):
        rows = pl.ds(pl.multiple_of(lax.rem(where[0] + s, 4) * 64, 64), 64)
        for ch in range(2):
            out[ch] = keep[ch, rows, :] + got[ch, rows, :]


def mix_kernel(where, keep, got, o0, o1, o2, o3):
    for s, out in enumerate((o0, o1, o2, o3)):
        j = lax.rem(where[3] + s, 4)
        out[...] = keep[j] + got[j]


def sum_kernel(where, g0, g1, g2, g3, own, out):
    odd = lax.rem(where[1], 2)
    for target, half in ((own, odd), (out, 1 - odd)):
        rows = pl.ds(pl.multiple_of(half * 32, 32), 32)
        for ch in range(2):
            target[ch] = (g0[ch, rows, :] + g1[ch, rows, :]) + (g2[ch, rows, :] + g3[ch, rows, :])


def rows_kernel(where, f0, f1, f2, f3, out):
    for s, f in enumerate((f0, f1, f2, f3)):
        out[pl.ds(pl.multiple_of(lax.rem(where[0] + 4 - s, 4) * 32, 32), 32), :] = f[128:, :]


def light_kernel(where, positions, near, far, out, padded):
    padded[:32, :] = jnp.zeros((32, N), f32)
    padded[pl.ds(pl.multiple_of(32 + 128 * where[2], 32), 128), :] = near[...]
    padded[pl.ds(pl.multiple_of(32 + 128 * (1 - where[2]), 32), 128), :] = far[...]
    padded[288:328, :] = jnp.zeros((40, N), f32)
    first = 256 * where[2] + 64 * where[0] + 32 * lax.rem(where[1], 2)
    total = jnp.zeros((32, SIDE), f32)
    for f in range(8):
        start = jnp.clip(first - positions[f, 0] + 32, 0, 288)
        base = start // 8 * 8
        rows = padded[pl.ds(pl.multiple_of(base, 8), 40), :]
        rows = pltpu.roll(rows, lax.rem(40 - (start - base), 40), 0)[:32]
        wide = jnp.concatenate([rows, jnp.zeros((32, N), f32)], axis=1)
        total = total + pltpu.roll(wide, positions[f, 1], 1)
    out[...] = total


def probe_sum_kernel(q0, q1, q2, q3, p0, p1, p2, p3, power):
    power[...] = (q0[256:, :] + q1[256:, :]) + (q2[256:, :] + q3[256:, :])
    for s, p in enumerate((p0, p1, p2, p3)):
        rows = slice(64 * s, 64 * s + 64)
        p[...] = (q0[rows, :] + q1[rows, :]) + (q2[rows, :] + q3[rows, :])


def update_kernel(own, got, obj, light, out):
    scale = light[...] + damping
    for ch in range(2):
        out[ch] = obj[ch] + (own[ch] + got[ch]) / scale


def probe_kernel(q0, q1, mine, new):
    new[...] = mine[...] + (q0[:64, :] + q1[:64, :]) / (q0[64:, :] + q1[64:, :] + damping)


def block_kernel(where, n0, n1, n2, n3, q0, q1, q2, q3, power, out, q):
    for s, n in enumerate((n0, n1, n2, n3)):
        source = lax.rem(where[1] + 4 - s, 4)
        rows = pl.ds(pl.multiple_of(lax.rem(source, 2) * 32, 32), 32)
        for ch in range(2):
            out[source // 2, ch, rows, :] = n[ch]
    q[:64, :] = (q0[...] + q1[...]) + (q2[...] + q3[...])
    q[64:, :] = power[...]


def split_kernel(where, b0, b1, b2, b3, n0, n1, n2, n3, keep, send, half):
    y, c, x = where[0], where[2], where[3]
    for s, (b, n) in enumerate(((b0, n0), (b1, n1), (b2, n2), (b3, n3))):
        rows = pl.ds(pl.multiple_of(lax.rem(y + 4 - s, 4) * 64, 64), 64)
        for ch in range(2):
            keep[ch, rows, :] = b[c, ch]
            send[ch, rows, :] = b[1 - c, ch]
        half[pl.ds(pl.multiple_of(lax.rem(x + 4 - s, 4) * 64, 64), 64), :] = n[...]


def last_kernel(where, keep, got, half, other, tile, probe):
    c = where[2]
    for ch in range(2):
        tile[ch, pl.ds(pl.multiple_of(c * N, N), N), :] = keep[ch]
        tile[ch, pl.ds(pl.multiple_of((1 - c) * N, N), N), :] = got[ch]
    probe[c] = half[...]
    probe[1 - c] = other[...]


def shift(x, axis, n, s):
    return lax.ppermute(x, axis, [(i, (i + s) % n) for i in range(n)])


def local(object_field, probes, measured, positions, weights):
    rights, lefts, turn, turn_rows = tables()
    forward, inverse = (
        tuple(jnp.asarray(t) for t in (rights[i], lefts[i], turn, turn_rows)) for i in range(2)
    )
    y, zh, c, x = (lax.axis_index(a) for a in ("y", "zh", "c", "x"))
    where = jnp.stack([y, zh, c, x]).astype(jnp.int32)
    probe = probes[0]
    steps = (1, 2, 3)

    def ring(parts, axis, sign=1):
        return [parts[0]] + [shift(parts[s], axis, 4, sign * s) for s in steps]

    def swap(value):
        return shift(value, "c", 2, 1)

    def small(kernel, name, ins, outs, *operands):
        return call(kernel, name, ins, outs, flops=10**6, nbytes=MiB)(*operands)

    own = lax.dynamic_index_in_dim(probe, c, 0, False)
    message = jnp.concatenate([own, jnp.broadcast_to(weights[:, None], (8, N))], axis=0)
    near = ring([message] * 4, "zh")

    mine = zh // 2 == c
    offsets = jnp.where(mine, positions[0, 0], swap(positions[0, 0]))
    other_tile = swap(object_field)
    place = 4 * (zh % 2) + y // 2
    frames = [lax.dynamic_index_in_dim(measured[0, 0], place + 2 * i, 0, False) for i in (c, 1 - c)]

    plane = (N, N)
    patches, power, lit, psi0, intensity = call(
        first_kernel, "first", [S, S, S, S] + [V] * 9,
        [(2, 2) + plane, (2,) + plane, plane, (2, 2) + plane, (H, N)],
        [pltpu.VMEM((SIDE, SIDE), f32)], flops=5 * 10**9, nbytes=6 * MiB,
    )(where, offsets, positions[0, 0], weights, object_field, other_tile, frames[0], swap(frames[1]), probe, *forward)

    near = [lax.optimization_barrier((m, power))[0] for m in near[1:]]
    far = [swap(m) for m in near]
    *sums, psi, others = call(
        second_kernel, "second", [S, S] + [V] * 13,
        [(168, N)] * 4 + [(3, 2, 2) + plane, (3, 2) + plane],
        [pltpu.VMEM((2,) + plane, f32), pltpu.VMEM((128, N), f32)], flops=15 * 10**9, nbytes=10 * MiB, limit=24,
    )(where, weights, patches, probe, power, *near, *far, *forward)

    (factor,) = small(factor_kernel, "factor", [V] * 5, [(160, N)], *ring(sums, "y"), intensity)
    factors = ring([factor] * 4, "y")

    gkeep, gsend, chi = call(
        third_kernel, "third", [S, S] + [V] * 12,
        [(2, N, SIDE)] * 2 + [(2, 4, 2) + plane],
        [pltpu.VMEM((4, 128, N), f32), pltpu.VMEM((2, SIDE, SIDE), f32)],
        flops=20 * 10**9, nbytes=14 * MiB, limit=36,
    )(where, offsets, *factors, probe, others, psi0, psi, *inverse)
    keep, send = call(
        fourth_kernel, "fourth", [S, V, V, V], [(4, 320, N)] * 2, [pltpu.VMEM((2,) + plane, f32)],
        flops=10**7, nbytes=8 * MiB, limit=24,
    )(where, patches, chi, lit)

    part = (2, 32, SIDE)
    gswapped = swap(gsend)
    send = lax.optimization_barrier((send, gswapped))[0]
    folded = ring(small(fold_kernel, "fold", [S, V, V], [(2, 64, SIDE)] * 4, where, gkeep, gswapped), "y")
    mixed = ring(small(mix_kernel, "mix", [S, V, V], [(320, N)] * 4, where, keep, swap(send)), "x")

    (rows,) = small(rows_kernel, "rows", [S] + [V] * 4, [(128, N)], where, *factors)
    (light,) = call(
        light_kernel, "light", [S, S, V, V], [(32, SIDE)], [pltpu.VMEM((328, N), f32)],
        flops=10**6, nbytes=MiB,
    )(where, offsets, rows, swap(rows))
    targets = [
        lax.dynamic_index_in_dim(t.reshape(2, 16, 32, SIDE), 8 * c + 2 * y + zh % 2, 1, False)
        for t in (object_field, other_tile)
    ]
    target = jnp.where(mine, *targets)
    own_rows = lax.dynamic_slice(probe, (c, 64 * x, 0), (1, 64, N))[0]

    own, out = small(sum_kernel, "sum", [S] + [V] * 4, [part] * 2, where, *folded)
    got = lax.ppermute(out, "zh", [(0, 1), (1, 0), (2, 3), (3, 2)])
    *qs, e = small(probe_sum_kernel, "probe_sum", [V] * 4, [(64, N)] * 5, *mixed)
    (new,) = small(update_kernel, "update", [V] * 4, [part], own, got, target, light)
    block, q = small(
        block_kernel, "block", [S] + [V] * 9, [(2, 2, 64, SIDE), (128, N)],
        where, *ring([new] * 4, "zh"), *ring(qs, "zh", -1), e,
    )
    blocks = ring([block] * 4, "y")
    (chunk,) = small(probe_kernel, "probe", [V] * 3, [(64, N)], q, shift(q, "zl", 2, 1), own_rows)
    chunks = ring([chunk] * 4, "x")
    keep, send, half = small(
        split_kernel, "split", [S] + [V] * 8, [(2, N, SIDE)] * 2 + [plane], where, *blocks, *chunks
    )
    new_object, new_probe = small(
        last_kernel, "last", [S] + [V] * 4, [(2, SIDE, SIDE), (2,) + plane],
        where, keep, swap(send), half, swap(half),
    )
    return new_object, new_probe[None]


def solution(mesh):
    inner = Mesh(mesh.devices.reshape(4, 4, 2, 2, 4), ("y", "zh", "zl", "c", "x"))
    wave, ty, tx = ("y", "zh"), ("zl", "c"), "x"
    in_specs = (
        P(None, ty, tx),
        P(wave, None, None, None),
        P(ty, tx, None, None, None),
        P(ty, tx, None, None),
        P(wave),
    )
    out_specs = (P(None, ty, tx), P(wave, None, None, None))
    return jax.shard_map(local, mesh=inner, in_specs=in_specs, out_specs=out_specs, check_vma=False)
```

```python
import math

import jax
import jax.numpy as jnp
import ml_dtypes
import numpy as np
from jax import lax
from jax.experimental import pallas as pl
from jax.experimental.pallas import tpu as pltpu
from jax.sharding import Mesh
from jax.sharding import PartitionSpec as P

f32 = jnp.float32
bf16 = jnp.bfloat16
damping = 1.0
intensity_offset = 0.1
N = 256
H = 128
SIDE = 512
TALL = 264


def tables():
    k = np.arange(H)
    angle = 2.0 * math.pi / H * (np.outer(k, k) % H)
    c, s = np.cos(angle) / 16.0, -np.sin(angle) / 16.0
    forward, inverse = np.block([[c, -s], [s, c]]), np.block([[c, s], [-s, c]])

    def split(table, axis):
        high = table.astype(np.float32).astype(ml_dtypes.bfloat16)
        low = (table - high.astype(np.float64)).astype(np.float32).astype(ml_dtypes.bfloat16)
        return np.concatenate([high, high, low], axis=axis)

    turn = np.exp(-2j * math.pi * k / N)
    turn = np.stack([turn.real, turn.imag]).astype(np.float32)
    rows = np.broadcast_to(turn[:, :, None], (2, H, H)).copy()
    return [split(t.T, 0) for t in (forward, inverse)], [split(t, 1) for t in (forward, inverse)], turn, rows


def split_data(x, axis):
    high = x.astype(bf16)
    low = (x - high.astype(f32)).astype(bf16)
    return jnp.concatenate([high, low, high], axis=axis)


def cat(parts, axis):
    return jnp.concatenate(parts, axis=axis)


def twiddle(re, im, wr, wi):
    return re * wr - im * wi, re * wi + im * wr


def transform(re, im, right, left, turn, rows):
    a, b, ai, bi = re[:, :H], re[:, H:], im[:, :H], im[:, H:]
    o_re, o_im = twiddle(a - b, ai - bi, turn[0:1, :], turn[1:2, :])
    x = cat([cat([a + b, ai + bi], 1), cat([o_re, o_im], 1)], 0)
    x = jnp.dot(split_data(x, 1), right[...], preferred_element_type=f32)
    re, im = cat([x[:N, :H], x[N:, :H]], 1), cat([x[:N, H:], x[N:, H:]], 1)
    a, b, ai, bi = re[:H], re[H:], im[:H], im[H:]
    wr, wi = cat([rows[0]] * 2, 1), cat([rows[1]] * 2, 1)
    o_re, o_im = twiddle(a - b, ai - bi, wr, wi)
    x = cat([cat([a + b, ai + bi], 0), cat([o_re, o_im], 0)], 1)
    x = jnp.dot(left[...], split_data(x, 0), preferred_element_type=f32)
    return cat([x[:H, :N], x[:H, N:]], 0), cat([x[H:, :N], x[H:, N:]], 0)


def restore(re, im, right, left, turn, rows):
    x = cat([cat([re[:, :H], im[:, :H]], 1), cat([re[:, H:], im[:, H:]], 1)], 0)
    x = jnp.dot(split_data(x, 1), right[...], preferred_element_type=f32)
    o_re, o_im = twiddle(x[N:, :H], x[N:, H:], turn[0:1, :], -turn[1:2, :])
    e_re, e_im = x[:N, :H], x[:N, H:]
    re, im = cat([e_re + o_re, e_re - o_re], 1), cat([e_im + o_im, e_im - o_im], 1)
    x = cat([cat([re[:H], im[:H]], 0), cat([re[H:], im[H:]], 0)], 1)
    x = jnp.dot(left[...], split_data(x, 0), preferred_element_type=f32)
    wr, wi = cat([rows[0]] * 2, 1), -cat([rows[1]] * 2, 1)
    o_re, o_im = twiddle(x[:H, N:], x[H:, N:], wr, wi)
    e_re, e_im = x[:H, :N], x[H:, :N]
    return cat([e_re + o_re, e_re - o_re], 0), cat([e_im + o_im, e_im - o_im], 0)


def split_row(row):
    base = pl.multiple_of(jnp.minimum(row // 8 * 8, SIDE - TALL), 8)
    return base, row - base


def spec(space=pltpu.VMEM):
    return pl.BlockSpec(memory_space=space)


def call(kernel, name, ins, outs, scratch=(), flops=0, nbytes=0, limit=16):
    return pl.pallas_call(
        kernel,
        name=name,
        out_shape=[jax.ShapeDtypeStruct(o, f32) for o in outs],
        in_specs=ins,
        out_specs=[spec() for _ in outs],
        scratch_shapes=list(scratch),
        compiler_params=pltpu.CompilerParams(vmem_limit_bytes=limit * MiB),
        cost_estimate=pl.CostEstimate(flops=flops, bytes_accessed=nbytes, transcendentals=0),
    )


V = spec()
S = spec(pltpu.SMEM)
MiB = 1 << 20


def pick(frame, parity):
    i, r = lax.broadcasted_iota(jnp.int32, (H, N), 0), lax.broadcasted_iota(jnp.int32, (H, N), 1)
    pick_rows = jnp.where(r == 2 * i + parity, 1.0, 0.0).astype(bf16)
    r, j = lax.broadcasted_iota(jnp.int32, (N, N), 0), lax.broadcasted_iota(jnp.int32, (N, N), 1)
    pick_columns = jnp.where(r == jnp.where(j < H, 2 * j, 2 * j - (N - 1)), 1.0, 0.0).astype(bf16)
    rest = frame
    total = jnp.zeros((H, N), f32)
    for _ in range(3):
        part = rest.astype(bf16)
        rest = rest - part.astype(f32)
        part = jnp.dot(pick_rows, part, preferred_element_type=f32).astype(bf16)
        total = total + jnp.dot(part, pick_columns, preferred_element_type=f32)
    return total


def first_kernel(where, positions, own_positions, weight, obj, got, frame, got_frame, probe, right, left, turn, rows128,
                 patches, power, total, psi, intensity, squares):
    table = (right, left, turn, rows128)
    y, zh, c = where[0], where[1], where[2]
    mine = zh // 2 == c
    w = weight[0]
    first = 4 * lax.rem(zh, 2) + 2 * c

    def window(source, row, col):
        base, down = split_row(row)
        part = pltpu.roll(source[pl.ds(base, TALL), :], lax.rem(SIDE - col, SIDE), 1)[:, :N]
        return pltpu.roll(part, lax.rem(TALL - down, TALL), 0)[:N]

    def take(source):
        for f in range(2):
            for ch in range(2):
                patches[f, ch] = window(source.at[ch], positions[first + f, 0], positions[first + f, 1])

    @pl.when(mine)
    def _():
        take(obj)

    @pl.when(jnp.logical_not(mine))
    def _():
        take(got)

    for f in range(2):
        o_re, o_im = patches[f, 0], patches[f, 1]
        p_re, p_im = probe[0], probe[1]
        re, im = transform(p_re * o_re - p_im * o_im, p_re * o_im + p_im * o_re, *table)
        psi[f, 0] = re
        psi[f, 1] = im
        power[f] = w * (re * re + im * im)
    squares[...] = obj[0] * obj[0] + obj[1] * obj[1]
    lit = jnp.zeros((N, N), f32)
    for f in range(8):
        lit = lit + window(squares, own_positions[f, 0], own_positions[f, 1])
    total[...] = lit
    flag = jnp.full((1, N), zh // 2 - c, jnp.int32) == 0
    intensity[...] = pick(jnp.where(flag, frame[...], got_frame[...]), lax.rem(y, 2))


def more_waves(where, patches, arrivals, table, power, psi, probes):
    c = where[2]
    flag = jnp.full((1, N), c, jnp.int32) == 0
    mine = pl.ds(pl.multiple_of(128 * c, 128), 128)
    wsum = jnp.zeros((8, N), f32)
    light = jnp.zeros((128, N), f32)
    for i, (a, b) in enumerate(arrivals):
        own, other = a[:N, :], b[:N, :]
        p_re, p_im = jnp.where(flag, own, other), jnp.where(flag, other, own)
        probes[i, 0] = p_re
        probes[i, 1] = p_im
        wsum = wsum + a[N:, :]
        w = a[N:N + 1, :]
        for f in range(2):
            o_re, o_im = patches[f, 0], patches[f, 1]
            re, im = transform(p_re * o_re - p_im * o_im, p_re * o_im + p_im * o_re, *table)
            psi[i, f, 0] = re
            psi[i, f, 1] = im
            power[f] += w * (re * re + im * im)
        re, im = probes[i, 0, mine, :], probes[i, 1, mine, :]
        light = light + (re * re + im * im)
    return wsum, light


def second_kernel(where, weight, patches, probe, power0, a1, a2, a3, b1, b2, b3, right, left, turn, rows128,
                  out0, out1, out2, out3, psi, probes, power, lights):
    power[...] = power0[...]
    wsum, light = more_waves(
        where, patches, ((a1, b1), (a2, b2), (a3, b3)), (right, left, turn, rows128), power, psi, probes
    )
    wsum = wsum + weight[0]
    mine = pl.ds(pl.multiple_of(128 * where[2], 128), 128)
    re, im = probe[0, mine, :], probe[1, mine, :]
    lights[...] = light + (re * re + im * im)
    for s, out in enumerate((out0, out1, out2, out3)):
        j = lax.rem(where[0] + s, 4)
        out[:128, :] = power[j // 2, pl.ds(pl.multiple_of((j % 2) * 128, 128), 128), :]
        out[128:136, :] = wsum
        out[136:168, :] = lights[pl.ds(pl.multiple_of(32 * j, 32), 32), :]


def factor_kernel(m0, m1, m2, m3, measured, out):
    total = (m0[...] + m1[...]) + (m2[...] + m3[...])
    model = total[:128] / total[128:129]
    out[:128, :] = jnp.sqrt(measured[...]) / jnp.sqrt(model + intensity_offset) - 1.0
    out[128:, :] = total[136:]


def third_kernel(where, positions, f0, f1, f2, f3, probe, probes, psi0, psi, right, left, turn, rows128,
                 gkeep, gsend, chi, factor, canvas):
    table = (right, left, turn, rows128)
    y, zh, c = where[0], where[1], where[2]
    first = 4 * lax.rem(zh, 2) + 2 * c
    for s, f in enumerate((f0, f1, f2, f3)):
        factor[lax.rem(y + 4 - s, 4)] = f[:128, :]
    canvas[...] = jnp.zeros_like(canvas)
    waves = [(probe, psi0)] + [(probes.at[i], psi.at[i]) for i in range(3)]
    for f in range(2):
        fac = jnp.concatenate([factor[2 * f], factor[2 * f + 1]], axis=0)
        g_re = jnp.zeros((N, N), f32)
        g_im = jnp.zeros((N, N), f32)
        for i, (probe_ref, far) in enumerate(waves):
            re, im = restore(far[f, 0] * fac, far[f, 1] * fac, *table)
            p_re, p_im = probe_ref[0], probe_ref[1]
            g_re = g_re + (p_re * re + p_im * im)
            g_im = g_im + (p_re * im - p_im * re)
            chi[f, i, 0] = re
            chi[f, i, 1] = im
        base, down = split_row(positions[first + f, 0])
        col = positions[first + f, 1]
        for ch, g in enumerate((g_re, g_im)):
            tall = pltpu.roll(jnp.concatenate([g, jnp.zeros((TALL - N, N), f32)], axis=0), down, 0)
            wide = pltpu.roll(jnp.concatenate([tall, jnp.zeros((TALL, N), f32)], axis=1), col, 1)
            canvas[ch, pl.ds(base, TALL), :] += wide
    for ch in range(2):
        gkeep[ch] = canvas[ch, pl.ds(pl.multiple_of(c * N, N), N), :]
        gsend[ch] = canvas[ch, pl.ds(pl.multiple_of((1 - c) * N, N), N), :]


def fourth_kernel(where, patches, chi, lit, keep, send, q):
    c = where[2]
    for i in range(4):
        re, im = jnp.zeros((N, N), f32), jnp.zeros((N, N), f32)
        for f in range(2):
            o_re, o_im, a, b = patches[f, 0], patches[f, 1], chi[f, i, 0], chi[f, i, 1]
            re = re + (o_re * a + o_im * b)
            im = im + (o_re * b - o_im * a)
        q[0] = re
        q[1] = im
        for xc in range(4):
            keep[xc, 64 * i:64 * i + 64, :] = q[c, 64 * xc:64 * xc + 64, :]
            send[xc, 64 * i:64 * i + 64, :] = q[1 - c, 64 * xc:64 * xc + 64, :]
    for xc in range(4):
        keep[xc, 256:, :] = lit[64 * xc:64 * xc + 64, :]
        send[xc, 256:, :] = lit[64 * xc:64 * xc + 64, :]


def fold_kernel(where, keep, got, o0, o1, o2, o3):
    for s, out in enumerate((o0, o1, o2, o3)):
        rows = pl.ds(pl.multiple_of(lax.rem(where[0] + s, 4) * 64, 64), 64)
        for ch in range(2):
            out[ch] = keep[ch, rows, :] + got[ch, rows, :]


def mix_kernel(where, keep, got, o0, o1, o2, o3):
    for s, out in enumerate((o0, o1, o2, o3)):
        j = lax.rem(where[3] + s, 4)
        out[...] = keep[j] + got[j]


def sum_kernel(where, g0, g1, g2, g3, own, out):
    odd = lax.rem(where[1], 2)
    for target, half in ((own, odd), (out, 1 - odd)):
        rows = pl.ds(pl.multiple_of(half * 32, 32), 32)
        for ch in range(2):
            target[ch] = (g0[ch, rows, :] + g1[ch, rows, :]) + (g2[ch, rows, :] + g3[ch, rows, :])


def rows_kernel(where, f0, f1, f2, f3, out):
    for s, f in enumerate((f0, f1, f2, f3)):
        out[pl.ds(pl.multiple_of(lax.rem(where[0] + 4 - s, 4) * 32, 32), 32), :] = f[128:, :]


def light_kernel(where, positions, near, far, out, padded):
    padded[:32, :] = jnp.zeros((32, N), f32)
    padded[pl.ds(pl.multiple_of(32 + 128 * where[2], 32), 128), :] = near[...]
    padded[pl.ds(pl.multiple_of(32 + 128 * (1 - where[2]), 32), 128), :] = far[...]
    padded[288:328, :] = jnp.zeros((40, N), f32)
    first = 256 * where[2] + 64 * where[0] + 32 * lax.rem(where[1], 2)
    total = jnp.zeros((32, SIDE), f32)
    for f in range(8):
        start = jnp.clip(first - positions[f, 0] + 32, 0, 288)
        base = start // 8 * 8
        rows = padded[pl.ds(pl.multiple_of(base, 8), 40), :]
        rows = pltpu.roll(rows, lax.rem(40 - (start - base), 40), 0)[:32]
        wide = jnp.concatenate([rows, jnp.zeros((32, N), f32)], axis=1)
        total = total + pltpu.roll(wide, positions[f, 1], 1)
    out[...] = total


def probe_sum_kernel(q0, q1, q2, q3, p0, p1, p2, p3, power):
    power[...] = (q0[256:, :] + q1[256:, :]) + (q2[256:, :] + q3[256:, :])
    for s, p in enumerate((p0, p1, p2, p3)):
        rows = slice(64 * s, 64 * s + 64)
        p[...] = (q0[rows, :] + q1[rows, :]) + (q2[rows, :] + q3[rows, :])


def update_kernel(own, got, obj, light, out):
    scale = light[...] + damping
    for ch in range(2):
        out[ch] = obj[ch] + (own[ch] + got[ch]) / scale


def probe_kernel(q0, q1, mine, new):
    new[...] = mine[...] + (q0[:64, :] + q1[:64, :]) / (q0[64:, :] + q1[64:, :] + damping)


def block_kernel(where, n0, n1, n2, n3, q0, q1, q2, q3, power, out, q):
    for s, n in enumerate((n0, n1, n2, n3)):
        source = lax.rem(where[1] + 4 - s, 4)
        rows = pl.ds(pl.multiple_of(lax.rem(source, 2) * 32, 32), 32)
        for ch in range(2):
            out[source // 2, ch, rows, :] = n[ch]
    q[:64, :] = (q0[...] + q1[...]) + (q2[...] + q3[...])
    q[64:, :] = power[...]


def half_kernel(where, n0, n1, n2, n3, half):
    for s, n in enumerate((n0, n1, n2, n3)):
        half[pl.ds(pl.multiple_of(lax.rem(where[3] + 4 - s, 4) * 64, 64), 64), :] = n[...]


def send_kernel(where, b0, b1, b2, b3, send):
    for s, b in enumerate((b0, b1, b2, b3)):
        send[s] = b[1 - where[2]]


def last_kernel(where, b0, b1, b2, b3, got, half, other, tile, probe):
    y, c = where[0], where[2]
    for s, b in enumerate((b0, b1, b2, b3)):
        start = lax.rem(y + 4 - s, 4) * 64
        mine = pl.ds(pl.multiple_of(start + c * N, 64), 64)
        theirs = pl.ds(pl.multiple_of(start + (1 - c) * N, 64), 64)
        for ch in range(2):
            tile[ch, mine, :] = b[c, ch]
            tile[ch, theirs, :] = got[s, ch]
    probe[c] = half[...]
    probe[1 - c] = other[...]


def shift(x, axis, n, s):
    return lax.ppermute(x, axis, [(i, (i + s) % n) for i in range(n)])


def local(object_field, probes, measured, positions, weights):
    rights, lefts, turn, turn_rows = tables()
    forward, inverse = (
        tuple(jnp.asarray(t) for t in (rights[i], lefts[i], turn, turn_rows)) for i in range(2)
    )
    y, zh, c, x = (lax.axis_index(a) for a in ("y", "zh", "c", "x"))
    where = jnp.stack([y, zh, c, x]).astype(jnp.int32)
    probe = probes[0]
    steps = (1, 2, 3)

    def ring(parts, axis, sign=1):
        return [parts[0]] + [shift(parts[s], axis, 4, sign * s) for s in steps]

    def swap(value):
        return shift(value, "c", 2, 1)

    def small(kernel, name, ins, outs, *operands):
        return call(kernel, name, ins, outs, flops=10**6, nbytes=MiB)(*operands)

    own = lax.dynamic_index_in_dim(probe, c, 0, False)
    message = jnp.concatenate([own, jnp.broadcast_to(weights[:, None], (8, N))], axis=0)
    near = ring([message] * 4, "zh")

    mine = zh // 2 == c
    offsets = jnp.where(mine, positions[0, 0], swap(positions[0, 0]))
    other_tile = swap(object_field)
    place = 4 * (zh % 2) + y // 2
    frames = [lax.dynamic_index_in_dim(measured[0, 0], place + 2 * i, 0, False) for i in (c, 1 - c)]

    plane = (N, N)
    patches, power, lit, psi0, intensity = call(
        first_kernel, "first", [S, S, S, S] + [V] * 9,
        [(2, 2) + plane, (2,) + plane, plane, (2, 2) + plane, (H, N)],
        [pltpu.VMEM((SIDE, SIDE), f32)], flops=5 * 10**9, nbytes=6 * MiB,
    )(where, offsets, positions[0, 0], weights, object_field, other_tile, frames[0], swap(frames[1]), probe, *forward)

    near = [lax.optimization_barrier((m, power))[0] for m in near[1:]]
    far = [swap(m) for m in near]
    *sums, psi, others = call(
        second_kernel, "second", [S, S] + [V] * 13,
        [(168, N)] * 4 + [(3, 2, 2) + plane, (3, 2) + plane],
        [pltpu.VMEM((2,) + plane, f32), pltpu.VMEM((128, N), f32)], flops=15 * 10**9, nbytes=10 * MiB, limit=24,
    )(where, weights, patches, probe, power, *near, *far, *forward)

    (factor,) = small(factor_kernel, "factor", [V] * 5, [(160, N)], *ring(sums, "y"), intensity)
    factors = ring([factor] * 4, "y")

    gkeep, gsend, chi = call(
        third_kernel, "third", [S, S] + [V] * 12,
        [(2, N, SIDE)] * 2 + [(2, 4, 2) + plane],
        [pltpu.VMEM((4, 128, N), f32), pltpu.VMEM((2, SIDE, SIDE), f32)],
        flops=20 * 10**9, nbytes=14 * MiB, limit=36,
    )(where, offsets, *factors, probe, others, psi0, psi, *inverse)
    keep, send = call(
        fourth_kernel, "fourth", [S, V, V, V], [(4, 320, N)] * 2, [pltpu.VMEM((2,) + plane, f32)],
        flops=10**7, nbytes=8 * MiB, limit=24,
    )(where, patches, chi, lit)

    part = (2, 32, SIDE)
    gswapped = swap(gsend)
    send = lax.optimization_barrier((send, gswapped))[0]
    folded = ring(small(fold_kernel, "fold", [S, V, V], [(2, 64, SIDE)] * 4, where, gkeep, gswapped), "y")
    mixed = ring(small(mix_kernel, "mix", [S, V, V], [(320, N)] * 4, where, keep, swap(send)), "x")

    (rows,) = small(rows_kernel, "rows", [S] + [V] * 4, [(128, N)], where, *factors)
    (light,) = call(
        light_kernel, "light", [S, S, V, V], [(32, SIDE)], [pltpu.VMEM((328, N), f32)],
        flops=10**6, nbytes=MiB,
    )(where, offsets, rows, swap(rows))
    targets = [
        lax.dynamic_index_in_dim(t.reshape(2, 16, 32, SIDE), 8 * c + 2 * y + zh % 2, 1, False)
        for t in (object_field, other_tile)
    ]
    target = jnp.where(mine, *targets)
    own_rows = lax.dynamic_slice(probe, (c, 64 * x, 0), (1, 64, N))[0]

    own, out = small(sum_kernel, "sum", [S] + [V] * 4, [part] * 2, where, *folded)
    got = lax.ppermute(out, "zh", [(0, 1), (1, 0), (2, 3), (3, 2)])
    *qs, e = small(probe_sum_kernel, "probe_sum", [V] * 4, [(64, N)] * 5, *mixed)
    (new,) = small(update_kernel, "update", [V] * 4, [part], own, got, target, light)
    block, q = small(
        block_kernel, "block", [S] + [V] * 9, [(2, 2, 64, SIDE), (128, N)],
        where, *ring([new] * 4, "zh"), *ring(qs, "zh", -1), e,
    )
    blocks = ring([block] * 4, "y")
    (chunk,) = small(probe_kernel, "probe", [V] * 3, [(64, N)], q, shift(q, "zl", 2, 1), own_rows)
    chunks = ring([chunk] * 4, "x")
    (half,) = small(half_kernel, "half", [S] + [V] * 4, [plane], where, *chunks)
    blocks = lax.optimization_barrier((blocks, half))[0]
    (send,) = small(send_kernel, "send", [S] + [V] * 4, [(4, 2, 64, SIDE)], where, *blocks)
    new_object, new_probe = small(
        last_kernel, "last", [S] + [V] * 7, [(2, SIDE, SIDE), (2,) + plane],
        where, *blocks, swap(send), half, swap(half),
    )
    return new_object, new_probe[None]


def solution(mesh):
    inner = Mesh(mesh.devices.reshape(4, 4, 2, 2, 4), ("y", "zh", "zl", "c", "x"))
    wave, ty, tx = ("y", "zh"), ("zl", "c"), "x"
    in_specs = (
        P(None, ty, tx),
        P(wave, None, None, None),
        P(ty, tx, None, None, None),
        P(ty, tx, None, None),
        P(wave),
    )
    out_specs = (P(None, ty, tx), P(wave, None, None, None))
    return jax.shard_map(local, mesh=inner, in_specs=in_specs, out_specs=out_specs, check_vma=False)
```
